128 devices in a mesh: group: 4 (over y), shard: 32 (over x, z, core).
Axes of the slice: x: 4, y: 4, z: 4, core: 2. Of those that a mesh axis runs over, the one named last changes fastest.
Arguments:
- queries: bfloat16 [16384, 768], P(('group', 'shard')), may hold values from -12 to 12
- projection: bfloat16 [768, 768], replicated, may hold values from -0.21875 to 0.21875
- labels: bfloat16 [262144, 768], P(('group', 'shard')), may hold values from -6 to 6
- accumulator: float32 [262144], P(('group', 'shard')), may hold values from 0.01 to 4
- shortlist: int32 [16384, 32], P(('group', 'shard')), may hold values from 0 to 1023, all different within a row; in each aligned block of 128 rows (0 to 127, 128 to 255, ...) at most 8 rows name the same one
- positives: int32 [16384, 4], P(('group', 'shard')), may hold values from 0 to 8191
Outputs:
- updated_labels: bfloat16 [262144, 768], P(('group', 'shard'))
- updated_accumulator: float32 [262144], P(('group', 'shard'))
- projection_grad: float32 [768, 768], replicated
The draws below stay inside these ranges and needn't reach their ends.
Inputs may be any that keep to these rules, and one draw needn't show every extreme that they name: `shortlist`: each query names 32 different clusters. Among the 128 queries of one device no cluster is named more than 8 times, a bound that some block reaches.
All inputs are finite; a program needn't handle non-finite values.
Results may differ from the reference program's by a relative error of at most 0.0036.
The reference program's roundings to bfloat16 on the way (of `hidden`, `signal` and `query_grad`) count: a program that leaves them out, or rounds other values in their place, can miss the bound.
Values may be sent and summed in bfloat16 or wider, within the bound.
A program may use at most 192 MiB of HBM per device.

```python
import math
import jax
import jax.numpy as jnp
import numpy as np
from jax import lax

D = 768
LBL = 256
SHORT = 32
POS = 4
QD = 128
CL_DEV = 8
CLUSTERS = 1024
LABELS = 262144
QUERIES = 16384
MOST = 8
SLOTS = 1024


def draw_queries(key, part):
    key = jax.random.fold_in(key, 11)
    key_scale, key_main = jax.random.split(key, 2)
    column_scale = jnp.exp(jax.random.uniform(key_scale, (1, D), minval=math.log(0.3), maxval=math.log(3.0)))
    values = jax.random.normal(key_main, (QUERIES, D)) * column_scale
    return jnp.clip(values, -12.0, 12.0).astype(jnp.bfloat16)


def with_ends(result, own_key, least, high):
    place = [jax.random.randint(jax.random.fold_in(own_key, axis), (), 0, length) for axis, length in enumerate(result.shape)]
    main_axis = result.shape.index(max(result.shape))
    beside = place[:main_axis] + [(place[main_axis] + 1) % result.shape[main_axis]] + place[main_axis + 1:]
    return result.at[tuple(place)].set(least).at[tuple(beside)].set(high)


def block_levels(own_key, extent, cuts, smallest, largest):
    def one(dim, parts):
        steps = jax.random.uniform(jax.random.fold_in(jax.random.fold_in(own_key, 6), dim), (parts,), jnp.float32, smallest / len(cuts), largest / len(cuts))
        return jnp.repeat(jnp.exp(steps), extent[dim] // parts).reshape((-1,) + (1,) * (len(extent) - dim - 1))

    level = one(*cuts[0])
    for cut in cuts[1:]:
        level = level * one(*cut)
    return level


def deal_out(stream_key, own, number, rows, number_of, top, most, slope):
    sequence = jax.random.permutation(stream_key, number_of)
    packed, usual = shares(number_of, rows * top, most, slope, True), shares(number_of, rows * top, most, slope, False)
    places = jnp.arange(number_of)

    def named(lengths, rotation):
        used = int((lengths > 0).sum())
        fixed = max(1, used // 4)
        passed = fixed + (places - fixed + rotation * (used - fixed)) % max(1, number_of - fixed)
        return jnp.zeros((number_of,), jnp.int32).at[sequence[jnp.where(places < fixed, places, passed)]].set(jnp.asarray(lengths, jnp.int32))

    lengths = jnp.where(number % 4 == 0, named(packed, number // 4), named(usual, number - number // 4 - 1))
    mixed = jax.random.permutation(jax.random.fold_in(own, 3), number_of)
    source_of, receiver = mixed[0:number_of // 2 * 2:2], mixed[1:number_of // 2 * 2:2]
    slack = jnp.minimum(lengths[source_of] - 1, most - lengths[receiver]) // 2
    slack = jnp.where((source_of == sequence[0]) | (receiver == sequence[0]) | (lengths[receiver] == 0), 0, jnp.maximum(slack, 0))
    passed = jax.random.randint(jax.random.fold_in(own, 4), (number_of // 2,), 0, 1 << 20) % (slack + 1)
    lengths = lengths.at[source_of].add(-passed).at[receiver].add(passed)
    items = jnp.searchsorted(jnp.cumsum(lengths), jnp.arange(rows * top), side="right").astype(jnp.int32)
    listing = items.reshape(top, rows).T
    listing = listing[jax.random.permutation(jax.random.fold_in(own, 1), rows)]
    rotation = jax.random.randint(jax.random.fold_in(own, 2), (rows, 1), 0, top)
    return jnp.take_along_axis(listing, (jnp.arange(top)[None, :] + rotation) % top, axis=1)


def shares(count, total, bound, slope, full):
    weights = [(1 << 20) // math.isqrt(rank ** slope) + 1 for rank in range(1, count + 1)]
    largest = bound if full else min(bound, max(-(-total // count), total * weights[0] // sum(weights)))
    least = 1 if total - largest >= count - 1 else 0
    given, surplus = [largest] + [least] * (count - 1), total - largest - least * (count - 1)
    while surplus > 0:
        free = [i for i in range(1, count) if given[i] < largest] or [i for i in range(1, count) if given[i] < bound]
        pool, left = sum([weights[i] for i in free]), surplus
        for i in free:
            addition = min(bound - given[i], max(1, left * weights[i] // pool), surplus)
            given[i] = given[i] + addition
            surplus = surplus - addition
    return np.array(given)


def gaussian(rng, extent, width, reach, cuts=(), held_as=jnp.bfloat16):
    drawn = width * jax.random.normal(rng, extent, jnp.float32)
    if cuts:
        drawn = drawn * block_levels(rng, extent, cuts, -0.22, 0.18)
    return jnp.clip(drawn, -reach, reach).astype(held_as)


def setup_inputs(seed: int = 0) -> dict:
    seeds = jax.random.split(jax.random.key(seed), 7)
    queries = draw_queries(jax.random.fold_in(seeds[6], 71), 0)
    projection = gaussian(seeds[1], (D, D), D ** -0.5, 0.21875)
    labels = gaussian(seeds[2], (LABELS, D), 1.0, 6.0, ((0, 128),))
    accumulator = jnp.clip(jnp.exp(math.log(4.0) - 5.9914646 * jax.random.uniform(seeds[3], (LABELS,), jnp.float32) ** block_levels(seeds[3], (LABELS,), ((0, 128),), -0.2, 0.2)), 0.01, 4.0)
    shortlist_keys = jax.random.split(jax.random.fold_in(seeds[4], 1), QUERIES // QD)
    shortlist_turns = jax.random.permutation(jax.random.fold_in(seeds[4], 3), QUERIES // QD)
    shortlist = jax.vmap(lambda own, number: deal_out(jax.random.fold_in(seeds[4], 2), own, number, QD, CLUSTERS, SHORT, MOST, 2))(shortlist_keys, shortlist_turns).reshape((QUERIES, SHORT))
    positives = with_ends(jax.random.randint(seeds[5], (QUERIES, POS), 0, SHORT * LBL), jax.random.fold_in(seeds[5], 1), 0, (SHORT * LBL) - 1).astype(jnp.int32)
    return dict(queries=queries, projection=projection, labels=labels, accumulator=accumulator, shortlist=shortlist, positives=positives)


learn_rate = 1.0

def reference(queries, projection, labels, accumulator, shortlist, positives):
    query_total = queries.shape[0]
    features = queries.shape[1]
    logit_scale = 1.0 / math.sqrt(features)
    highest = lax.Precision.HIGHEST
    hidden = jnp.dot(queries, projection, preferred_element_type=jnp.float32).astype(jnp.bfloat16)
    requests = shortlist.reshape(-1).astype(jnp.int32)
    request_count = requests.shape[0]
    ordering = jnp.argsort(requests, stable=True).astype(jnp.int32)
    ordered = requests[ordering]
    first_seen = jnp.searchsorted(ordered, ordered, side='left').astype(jnp.int32)
    within = jnp.zeros((request_count,), jnp.int32).at[ordering].set(jnp.arange(request_count, dtype=jnp.int32) - first_seen)
    request_of = jnp.full((CLUSTERS * SLOTS,), request_count, jnp.int32)
    request_of = request_of.at[requests * SLOTS + within].set(jnp.arange(request_count, dtype=jnp.int32))
    hidden_pad = jnp.concatenate([hidden, jnp.zeros((1, features), jnp.bfloat16)], axis=0)
    positive_pad = jnp.concatenate([positives.astype(jnp.int32), jnp.full((1, POS), -1, jnp.int32)], axis=0)
    label_index = jnp.arange(LBL, dtype=jnp.int32)

    def one_block(summed, block_index):
        start = (block_index * CL_DEV).astype(jnp.int32)
        block_slots = lax.dynamic_slice_in_dim(request_of, start * SLOTS, CL_DEV * SLOTS).reshape(CL_DEV, SLOTS)
        filled = block_slots < request_count
        query_of = jnp.where(filled, block_slots // SHORT, query_total)
        column = jnp.where(filled, block_slots % SHORT, 0)
        row_vectors = hidden_pad[query_of].astype(jnp.float32)
        label_slab = lax.dynamic_slice_in_dim(labels, start * LBL, CL_DEV * LBL).reshape(CL_DEV, LBL, features).astype(jnp.float32)
        scores = jnp.einsum('csd,cld->csl', row_vectors, label_slab, precision=highest) * logit_scale
        local_pos = positive_pad[query_of] - column[..., None] * LBL
        target = jnp.any(local_pos[..., None] == label_index, axis=2).astype(jnp.float32)
        signal = (jax.nn.sigmoid(scores) - target).astype(jnp.bfloat16)
        label_grad = jnp.einsum('csl,csd->cld', signal.astype(jnp.float32), row_vectors, precision=highest) * logit_scale
        old_sums = lax.dynamic_slice_in_dim(accumulator, start * LBL, CL_DEV * LBL).reshape(CL_DEV, LBL)
        new_sums = old_sums + lax.optimization_barrier(jnp.mean(label_grad * label_grad, axis=2))
        updated = (label_slab - learn_rate * label_grad / jnp.sqrt(new_sums)[..., None]).astype(jnp.bfloat16)
        query_grad = (jnp.einsum('csl,cld->csd', signal.astype(jnp.float32), label_slab, precision=highest) * logit_scale).astype(jnp.bfloat16)
        summed = summed.at[query_of.reshape(-1)].add(query_grad.reshape(-1, features).astype(jnp.float32))
        return (summed, (updated, new_sums))
    start_sum = jnp.zeros((query_total + 1, features), jnp.float32)
    block_count = CLUSTERS // CL_DEV
    summed, (updated, new_sums) = lax.scan(one_block, start_sum, jnp.arange(block_count, dtype=jnp.int32))
    proj_sum = jnp.dot(queries.astype(jnp.float32).T, summed[:query_total], precision=highest)
    factor = jnp.minimum(1.0, features / jnp.sqrt(jnp.sum(proj_sum * proj_sum) + 1e-06))
    return (updated.reshape(LABELS, features), new_sums.reshape(LABELS), proj_sum * factor)
```

```python
import functools
import math

import jax
import jax.numpy as jnp
from jax import lax
from jax.experimental import pallas as pl
from jax.experimental.pallas import tpu as pltpu
from jax.sharding import PartitionSpec as P

MESH = pl.DeviceIdType.MESH
LBL = 256
QD = 128
D = 768
CL = 8
W = 8
BF = jnp.bfloat16
F32 = jnp.float32
ORDERS = ((0, 1, 2), (1, 2, 0), (2, 0, 1))
OFF = (0, -1, 1, 2)
GROUP = 16


def arrival(offset):
    place = {0: 0, 3: 1, 1: 2, 2: 3}
    worst = 0
    for order in ORDERS:
        third, second = place[offset[order[2]]], place[offset[order[1]]]
        if third == 0:
            tick = (0, 1, 1, 2)[second]
        else:
            tick = (3 + second) if third in (1, 2) else 4 + second
        worst = max(worst, tick)
    return worst


CHIPS = sorted(
    [(a, b, c) for a in range(4) for b in range(4) for c in range(4)],
    key=lambda o: (arrival(o), o),
)


def dot(a, b, ca=1, cb=0):
    return lax.dot_general(a, b, (((ca,), (cb,)), ((), ())), preferred_element_type=F32)


def split(value):
    high = value.astype(BF)
    return high, (value - high.astype(F32)).astype(BF)


def kernel(
    q_ref, meta_ref, p_ref, tri_ref, acc_ref, l_hbm,
    new_hbm, sums_ref, proj_ref,
    gq, gm, lab, lp, lt, total, rows, cp, cd, mk, mc, pj, rb0, rb1, rb2, rb3, s1, s2, g1, full, stage,
    sem_l, sem_o,
    qs, qr, ms, mr, bs, br, bms, bmr, rs, rr,
):
    y = lax.axis_index("group")
    s = lax.axis_index("shard")
    x, z, k = s // 8, (s // 2) % 4, s % 2
    here = (x, y, z)
    scale = 1.0 / math.sqrt(D)

    def device(c, core):
        return (c[1], (c[0] * 4 + c[2]) * 2 + core)

    def shifted(axis, r):
        c = list(here)
        c[axis] = (c[axis] + r + 4) % 4
        return device(c, k)

    sibling = device(here, 1 - k)

    pending = []

    def remote(src, dst, ssem, rsem, target):
        copy = pltpu.make_async_remote_copy(
            src_ref=src, dst_ref=dst, send_sem=ssem, recv_sem=rsem,
            device_id=target, device_id_type=MESH,
        )
        copy.start()
        pending.append((src, ssem))

    def arrived(dst, rsem):
        pltpu.make_async_remote_copy(
            src_ref=dst, dst_ref=dst, send_sem=rsem, recv_sem=rsem,
            device_id=sibling, device_id_type=MESH,
        ).wait_recv()

    barrier = pltpu.get_barrier_semaphore()
    for axis in range(3):
        for r in (1, 2, 3):
            pl.semaphore_signal(barrier, inc=1, device_id=shifted(axis, r), device_id_type=MESH)
    pl.semaphore_signal(barrier, inc=1, device_id=sibling, device_id_type=MESH)
    pl.semaphore_wait(barrier, 10)

    load = pltpu.make_async_copy(l_hbm, lab, sem_l)
    load.start()

    at = [[here[a] for a in order] for order in ORDERS]

    def near(t, phase, i):
        return (at[t][phase] + OFF[i] + 4) % 4

    for t in range(3):
        i1, i2, i3 = at[t]
        gm[t, k, i3, i2, i1] = meta_ref[t]
        gq[t, k, i3, i2, i1] = q_ref[:, t * 256:(t + 1) * 256]

    def meta_phase(t, phase, ref):
        for r in (1, 2, 3):
            remote(ref, ref, ms.at[t, phase, r - 1], mr.at[t, phase, r - 1], shifted(ORDERS[t][phase], r))

    def meta_wait(t, phase, ref_of):
        for r in (1, 2, 3):
            arrived(ref_of((at[t][phase] - r + 4) % 4), mr.at[t, phase, r - 1])

    def both_ways(t, phase, n, ref):
        for way, r in ((0, 1), (1, -1)):
            remote(ref, ref, qs.at[t, n, way], qr.at[t, n, way], shifted(ORDERS[t][phase], r))

    def onward(t, phase, n, way, ref, half):
        arrived(ref, qr.at[t, n, way])
        part = half(ref, way)
        r = 1 if way == 0 else -1
        remote(part, part, qs.at[t, n + 1, way], qr.at[t, n + 1, way], shifted(ORDERS[t][phase], r))

    def far(t, n, ref, half):
        for way in (0, 1):
            arrived(half(ref, way), qr.at[t, n + 1, way])

    def row_half(ref, way):
        return ref.at[pl.ds(64 * way, 64)]

    def line_half(ref, way):
        return ref.at[pl.ds(2 * way, 2)]

    def line(t, r3, j):
        return gq.at[t, k, near(t, 2, r3), near(t, 1, j)]

    def to_sibling(t, r3, j):
        ref = line(t, r3, j)
        remote(ref, ref, bs.at[t, r3, j], br.at[t, r3, j], sibling)

    def from_sibling(t, r3, j):
        arrived(gq.at[t, 1 - k, near(t, 2, r3), near(t, 1, j)], br.at[t, r3, j])

    T3 = range(3)
    for t in T3:
        i1, i2, i3 = at[t]
        meta_phase(t, 0, gm.at[t, k, i3, i2, i1])
    for t in T3:
        i1, i2, i3 = at[t]
        both_ways(t, 0, 0, gq.at[t, k, i3, i2, i1])

    load.wait()

    def prepare(c, _):
        here_l = pl.ds(pl.multiple_of(c * LBL, LBL), LBL)
        slab = lab[here_l, :]
        lp[here_l, :] = dot(slab, p_ref[...], 1, 1).astype(BF)
        lt[:, here_l] = slab.T
        return 0

    for t in T3:
        i1, i2, i3 = at[t]
        onward(t, 0, 0, 0, gq.at[t, k, i3, i2, near(t, 0, 1)], row_half)
        onward(t, 0, 0, 1, gq.at[t, k, i3, i2, near(t, 0, 2)], row_half)
    for t in T3:
        i1, i2, i3 = at[t]
        meta_wait(t, 0, lambda i: gm.at[t, k, i3, i2, i])
        meta_phase(t, 1, gm.at[t, k, i3, i2])
    for t in T3:
        i1, i2, i3 = at[t]
        far(t, 0, gq.at[t, k, i3, i2, near(t, 0, 3)], row_half)
        both_ways(t, 1, 2, line(t, 0, 0))
        both_ways(t, 2, 4, line(t, 0, 0))
        to_sibling(t, 0, 0)
    lax.fori_loop(0, 2, prepare, 0)
    for t in T3:
        i1, i2, i3 = at[t]
        meta_wait(t, 1, lambda i: gm.at[t, k, i3, i])
        meta_phase(t, 2, gm.at[t, k, i3])
        remote(gm.at[t, k, i3], gm.at[t, k, i3], bms.at[t, 0], bmr.at[t, 0], sibling)
    lax.fori_loop(2, 4, prepare, 0)
    for way in (0, 1):
        for t in T3:
            j = way + 1
            onward(t, 1, 2, way, line(t, 0, j), line_half)
            both_ways(t, 2, 4 + 2 * j, line(t, 0, j))
            to_sibling(t, 0, j)
    lax.fori_loop(4, 6, prepare, 0)
    for t in T3:
        far(t, 2, line(t, 0, 3), line_half)
        both_ways(t, 2, 10, line(t, 0, 3))
        to_sibling(t, 0, 3)
    for t in T3:
        meta_wait(t, 2, lambda i: gm.at[t, k, i])
        for r in (1, 2, 3):
            ref = gm.at[t, k, (at[t][2] + r) % 4]
            remote(ref, ref, bms.at[t, r], bmr.at[t, r], sibling)
    lax.fori_loop(6, 8, prepare, 0)
    total[...] = jnp.zeros_like(total)
    for t in T3:
        for r in range(4):
            arrived(gm.at[t, 1 - k, (at[t][2] + r) % 4], bmr.at[t, r])

    number = y * 32 + s
    first = number * CL
    octave = first // 128
    base = (128 + first % 128).astype(F32)
    power = lax.shift_left(jnp.int32(1), octave.astype(jnp.int32)).astype(F32)

    def place_of(group, i):
        words = []
        for h in range(4):
            word = 0
            for n in range(4):
                o = CHIPS[group * GROUP + h * 4 + n]
                word |= (o[0] + 4 * o[1] + 16 * o[2]) << (6 * n)
            words.append(word)
        h, n = i // 4, i % 4
        word = jnp.where(h == 0, words[0], jnp.where(h == 1, words[1], jnp.where(h == 2, words[2], words[3])))
        code = lax.shift_right_logical(word.astype(jnp.int32), (6 * n).astype(jnp.int32))
        cx, cy, cz = code % 4, (code // 4) % 4, (code // 16) % 4
        return ((x + cx) % 4, (y + cy) % 4, (z + cz) % 4)

    def indices(c, t):
        a1, a2, a3 = ORDERS[t]
        return c[a3], c[a2], c[a1]

    def pair(ref, c, t):
        n3, n2, n1 = indices(c, t)
        return ref[t, 0, n3, n2, n1], ref[t, 1, n3, n2, n1]

    lane = lax.broadcasted_iota(jnp.int32, (16, 256), 1)
    sub = lax.broadcasted_iota(jnp.int32, (16, 256), 0)
    own_slot = jnp.where(sub // W == lane // QD, sub % W, -2).astype(F32)
    own_cluster = (
        lax.broadcasted_iota(jnp.int32, (CL, 128), 0) == lax.broadcasted_iota(jnp.int32, (CL, 128), 1) // 16
    )
    lane_chip = lax.broadcasted_iota(jnp.int32, (8, 128), 1) // 16

    def group_work(group):
        def names(i, _):
            c = place_of(group, i)
            a0, a1 = pair(gm, c, 0)
            b0, b1 = pair(gm, c, 1)
            ids = jnp.concatenate(
                [jnp.concatenate([a0, b0], axis=0), jnp.concatenate([a1, b1], axis=0)], axis=1
            ).astype(F32)
            column = lax.broadcasted_iota(jnp.int32, (32, 256), 0).astype(F32) + 1.0
            found = []
            for n in range(CL):
                found.append(jnp.sum(jnp.where(ids == (base + n) * power, column, 0.0), axis=0, keepdims=True))
            cp[pl.ds(pl.multiple_of(i * CL, CL), CL), :] = jnp.concatenate(found, axis=0)
            return 0

        lax.fori_loop(0, GROUP, names, 0)
        picked = cp[...] > 0.0
        rank = dot(jnp.where(picked, 1.0, 0.0).astype(BF), tri_ref[...])
        cd[...] = jnp.where(picked, rank, -1.0)

        def choose(i, _):
            c = place_of(group, i)
            here_c = pl.ds(pl.multiple_of(i * CL, CL), CL)
            code = cd[here_c, :]
            onehot = jnp.concatenate(
                [jnp.where(code[n:n + 1, :] == own_slot, 1.0, 0.0).astype(BF) for n in range(CL)], axis=0
            )
            m0, m1 = pair(gm, c, 2)
            marks = jnp.concatenate([m0, m1], axis=1).astype(F32)
            column = cp[here_c, :]
            shifted_marks = jnp.concatenate(
                [jnp.where(marks[n:n + 1, :] == column, marks[4 + n:5 + n, :], 0.0) for n in range(4)], axis=0
            ).astype(BF)
            spread = dot(shifted_marks, onehot, 1, 1)
            mk[i] = jnp.concatenate(
                [
                    jnp.sum(jnp.where(own_cluster, spread[n * CL:(n + 1) * CL, :], 0.0), axis=0, keepdims=True)
                    for n in range(4)
                ]
                + [jnp.zeros((4, 128), F32)],
                axis=0,
            )
            at_row = pl.ds(pl.multiple_of(i * 16, 16), 16)
            for t in T3:
                q0, q1 = pair(gq, c, t)
                got = dot(onehot, jnp.concatenate([q0, q1], axis=0)).astype(BF)
                for n in range(CL):
                    rows[n, at_row, t * 256:(t + 1) * 256] = got[n * 16:(n + 1) * 16, :]
            return 0

        lax.fori_loop(0, GROUP, choose, 0)
        for h in range(GROUP // 8):
            for n in range(CL):
                line_marks = jnp.zeros((8, 128), F32)
                for i in range(8):
                    turned = pltpu.roll(mk[h * 8 + i], (16 * (i - n)) % 128, 1)
                    line_marks = jnp.where(lane_chip == i, turned, line_marks)
                mc[n, :, h * 128:(h + 1) * 128] = line_marks

        def cluster(n, _):
            here_l = pl.ds(pl.multiple_of(n * LBL, LBL), LBL)
            r = rows[n]
            scores = dot(lp[here_l, :], r, 1, 1) * scale
            label = lax.broadcasted_iota(jnp.int32, (LBL, GROUP * 16), 0).astype(F32) + 1.0
            m = mc[n]
            hit = (m[0:1] == label) | (m[1:2] == label) | (m[2:3] == label) | (m[3:4] == label)
            signal = 1.0 / (1.0 + jnp.exp(-scores)) - jnp.where(hit, 1.0, 0.0)
            total[here_l, :] += dot(signal.astype(BF), r)
            return 0

        lax.fori_loop(0, CL, cluster, 0)

    def lines_after(j):
        for way in (0, 1):
            for t in T3:
                onward(t, 2, 4 + 2 * j, way, line(t, 1 + way, j), line_half)
                to_sibling(t, 1 + way, j)

    def far_after(j):
        for t in T3:
            far(t, 4 + 2 * j, line(t, 3, j), line_half)
            to_sibling(t, 3, j)

    def sibling_after(r3s, j):
        for t in T3:
            for r3 in r3s:
                from_sibling(t, r3, j)

    sibling_after((0,), 0)
    sibling_after((0,), 1)
    sibling_after((0,), 2)
    sibling_after((0,), 3)
    lines_after(0)
    lines_after(1)
    far_after(0)
    sibling_after((1, 2), 0)
    sibling_after((1, 2), 1)
    sibling_after((3,), 0)
    group_work(0)
    lines_after(2)
    far_after(1)
    sibling_after((1, 2), 2)
    sibling_after((3,), 1)
    group_work(1)
    lines_after(3)
    far_after(2)
    sibling_after((1, 2), 3)
    sibling_after((3,), 2)
    group_work(2)
    far_after(3)
    sibling_after((3,), 3)
    group_work(3)

    def project(half):
        at_half = pl.ds(pl.multiple_of(half * 384, 128), 384)

        def step(n, _):
            here_l = pl.ds(pl.multiple_of(n * LBL, LBL), LBL)
            high, low = split(total[here_l, :])
            left = lt[at_half, here_l]
            add = dot(left, high) + dot(left, low)
            pj[at_half, :] = jnp.where(n == 0, add, pj[at_half, :] + add)
            return 0

        lax.fori_loop(0, CL, step, 0)

    other_half = pl.ds(pl.multiple_of((1 - k) * 384, 128), 384)
    own_half = pl.ds(pl.multiple_of(k * 384, 128), 384)
    project(1 - k)
    remote(pj.at[other_half], rb0, rs.at[0], rr.at[0], sibling)
    project(k)

    eye = lax.broadcasted_iota(jnp.int32, (128, 128), 0) == lax.broadcasted_iota(jnp.int32, (128, 128), 1)

    def adagrad(n, _):
        here_l = pl.ds(pl.multiple_of(n * LBL, LBL), LBL)
        high, low = split(total[here_l, :])
        grad = (dot(high, p_ref[...]) + dot(low, p_ref[...])) * scale
        mean = jnp.sum(grad * grad, axis=1, keepdims=True) * (1.0 / D)
        old = jnp.concatenate(
            [
                jnp.sum(jnp.where(eye, acc_ref[pl.ds(n * 2 + h, 1), :], 0.0), axis=1, keepdims=True)
                for h in range(2)
            ],
            axis=0,
        )
        sums = old + mean
        for h in range(2):
            sums_ref[pl.ds(n * 2 + h, 1), :] = jnp.sum(
                jnp.where(eye, sums[h * 128:(h + 1) * 128], 0.0), axis=0, keepdims=True
            )
        stage[here_l, :] = (lab[here_l, :].astype(F32) - grad * (1.0 / jnp.sqrt(sums))).astype(BF)
        return 0

    lax.fori_loop(0, 1, adagrad, 0)
    arrived(rb0, rr.at[0])
    pj[own_half, :] += rb0[...]

    def cols(t):
        return pl.ds(t * 256, 256)

    def exchange(n, t, phase, src_of, dst_of):
        for r in (1, 2, 3):
            slot = 1 + n * 9 + t * 3 + r - 1
            remote(src_of(r), dst_of(r), rs.at[slot], rr.at[slot], shifted(ORDERS[t][phase], r))

    def exchanged(n, t, phase, dst_of):
        for r in (1, 2, 3):
            slot = 1 + n * 9 + t * 3 + r - 1
            arrived(dst_of(r, (at[t][phase] - r + 4) % 4), rr.at[slot])

    def piece(i):
        return pl.ds(pl.multiple_of(k * 384 + i * 96, 32), 96)

    for t in T3:
        exchange(0, t, 0, lambda r: pj.at[piece((at[t][0] + r) % 4), cols(t)], lambda r: rb1.at[t, r - 1])
    lax.fori_loop(1, 4, adagrad, 0)
    for t in T3:
        exchanged(0, t, 0, lambda r, i: rb1.at[t, r - 1])
        s1[t] = pj[piece(at[t][0]), cols(t)] + rb1[t, 0] + rb1[t, 1] + rb1[t, 2]
        exchange(
            1, t, 1,
            lambda r: s1.at[t, pl.ds(pl.multiple_of((at[t][1] + r) % 4 * 24, 8), 24)],
            lambda r: rb2.at[t, r - 1],
        )
    lax.fori_loop(4, 5, adagrad, 0)
    for t in T3:
        exchanged(1, t, 1, lambda r, i: rb2.at[t, r - 1])
        s2[t] = s1[t, pl.ds(pl.multiple_of(at[t][1] * 24, 8), 24)] + rb2[t, 0] + rb2[t, 1] + rb2[t, 2]
        rb3[t, at[t][2]] = s2[t]
        exchange(2, t, 2, lambda r: s2.at[t], lambda r: rb3.at[t, at[t][2]])
    lax.fori_loop(5, 6, adagrad, 0)
    for t in T3:
        exchanged(2, t, 2, lambda r, i: rb3.at[t, i])
        mine = pl.ds(pl.multiple_of(at[t][1] * 24, 8), 24)
        g1[t, mine] = (rb3[t, 0] + rb3[t, 1]) + (rb3[t, 2] + rb3[t, 3])
        exchange(3, t, 1, lambda r: g1.at[t, mine], lambda r: g1.at[t, mine])
    lax.fori_loop(6, 7, adagrad, 0)
    for t in T3:
        exchanged(3, t, 1, lambda r, i: g1.at[t, pl.ds(pl.multiple_of(i * 24, 8), 24)])
        full[piece(at[t][0]), cols(t)] = g1[t]
        exchange(4, t, 0, lambda r: g1.at[t], lambda r: full.at[piece(at[t][0]), cols(t)])
    lax.fori_loop(7, 8, adagrad, 0)
    store = pltpu.make_async_copy(stage, new_hbm, sem_o)
    store.start()
    for t in T3:
        exchanged(4, t, 0, lambda r, i: full.at[piece(i), cols(t)])
    remote(full.at[own_half], full.at[own_half], rs.at[46], rr.at[46], sibling)
    arrived(full.at[other_half], rr.at[46])

    squares = jnp.sum(full[...] * full[...]) * (scale * scale)
    factor = jnp.minimum(1.0, D / jnp.sqrt(squares + 1e-06)) * scale
    proj_ref[...] = full[...] * factor

    store.wait()
    for src, ssem in pending:
        pltpu.make_async_remote_copy(
            src_ref=src, dst_ref=src, send_sem=ssem, recv_sem=ssem,
            device_id=sibling, device_id_type=MESH,
        ).wait_send()


def on_device(queries, projection, labels, accumulator, shortlist, positives):
    ids = shortlist.astype(jnp.int32)
    codes = lax.shift_left(128 + ids % 128, ids // 128).T
    marks = jnp.concatenate([positives // LBL + 1, positives % LBL + 1], axis=1).T
    meta = jnp.concatenate([codes, marks, jnp.zeros((8, QD), jnp.int32)], axis=0).astype(BF).reshape(3, 16, QD)
    ordinal = jnp.arange(2 * QD)
    tri = (
        (ordinal[:, None] < ordinal[None, :]) & (ordinal[:, None] // QD == ordinal[None, :] // QD)
    ).astype(BF)
    vmem = pl.BlockSpec(memory_space=pltpu.VMEM)
    hbm = pl.BlockSpec(memory_space=pl.ANY)
    dma = pltpu.SemaphoreType.DMA
    new_labels, sums, proj = pl.pallas_call(
        kernel,
        out_shape=(
            jax.ShapeDtypeStruct((CL * LBL, D), BF),
            jax.ShapeDtypeStruct((16, 128), F32),
            jax.ShapeDtypeStruct((D, D), F32),
        ),
        in_specs=[vmem] * 5 + [hbm],
        out_specs=(hbm, vmem, vmem),
        scratch_shapes=[
            pltpu.VMEM((3, 2, 4, 4, 4, QD, 256), BF),
            pltpu.VMEM((3, 2, 4, 4, 4, 16, QD), BF),
            pltpu.VMEM((CL * LBL, D), BF),
            pltpu.VMEM((CL * LBL, D), BF),
            pltpu.VMEM((D, CL * LBL), BF),
            pltpu.VMEM((CL * LBL, D), F32),
            pltpu.VMEM((CL, GROUP * 16, D), BF),
            pltpu.VMEM((GROUP * CL, 256), F32),
            pltpu.VMEM((GROUP * CL, 256), F32),
            pltpu.VMEM((GROUP, 8, 128), F32),
            pltpu.VMEM((CL, 8, GROUP * 16), F32),
            pltpu.VMEM((D, D), F32),
            pltpu.VMEM((384, D), F32),
            pltpu.VMEM((3, 3, 96, 256), F32),
            pltpu.VMEM((3, 3, 24, 256), F32),
            pltpu.VMEM((3, 4, 24, 256), F32),
            pltpu.VMEM((3, 96, 256), F32),
            pltpu.VMEM((3, 24, 256), F32),
            pltpu.VMEM((3, 96, 256), F32),
            pltpu.VMEM((D, D), F32),
            pltpu.VMEM((CL * LBL, D), BF),
            dma, dma,
            dma((3, 12, 2)), dma((3, 12, 2)),
            dma((3, 3, 3)), dma((3, 3, 3)),
            dma((3, 4, 4)), dma((3, 4, 4)),
            dma((3, 4)), dma((3, 4)),
            dma((47,)), dma((47,)),
        ],
        compiler_params=pltpu.CompilerParams(
            collective_id=0, has_side_effects=True, vmem_limit_bytes=63 * 1024 * 1024
        ),
        cost_estimate=pl.CostEstimate(flops=20 * 10**9, bytes_accessed=20 * 10**6, transcendentals=0),
    )(queries, meta, projection, tri, accumulator.reshape(16, 128), labels)
    return new_labels, sums.reshape(-1), proj.T


def solution(mesh):
    in_specs = (
        P(("group", "shard"), None),
        P(),
        P(("group", "shard"), None),
        P(("group", "shard")),
        P(("group", "shard"), None),
        P(("group", "shard"), None),
    )
    out_specs = (P(("group", "shard"), None), P(("group", "shard")), P())
    return jax.shard_map(
        on_device, mesh=mesh, in_specs=in_specs, out_specs=out_specs, check_vma=False
    )
```

```python
import functools
import math

import jax
import jax.numpy as jnp
from jax import lax
from jax.experimental import pallas as pl
from jax.experimental.pallas import tpu as pltpu
from jax.sharding import PartitionSpec as P

MESH = pl.DeviceIdType.MESH
LBL = 256
QD = 128
D = 768
CL = 8
W = 8
BF = jnp.bfloat16
F32 = jnp.float32
ORDERS = ((0, 1, 2), (1, 2, 0), (2, 0, 1))
PLACE = {1: 1, 2: 3, 3: 2}
GROUP = 16
GROUPS = 4


def arrival(place):
    worst = 0
    for order in ORDERS:
        third, second = place[order[2]], place[order[1]]
        if third == 0:
            tick = (0, 1, 1, 2)[second]
        else:
            tick = (3 + second) if third in (1, 2) else 4 + second
        worst = max(worst, tick)
    return worst


CHIPS = sorted(
    [(a, b, c) for a in range(4) for b in range(4) for c in range(4)],
    key=lambda o: (arrival(o), o),
)


def dot(a, b, ca=1, cb=0):
    return lax.dot_general(a, b, (((ca,), (cb,)), ((), ())), preferred_element_type=F32)


def split(value):
    high = value.astype(BF)
    return high, (value - high.astype(F32)).astype(BF)


def kernel(
    q_ref, meta_ref, p_ref, acc_ref, l_hbm,
    new_hbm, sums_ref, proj_ref, factor_ref,
    gq, gm, lab, lp, lt, total, rows, cp, cd, oh, mk, mc, pj, rb0, sb, rb1, rb2, rb3, s1, s2, g1, g1b, full,
    sem_l, sem_o,
    qs, qr, ms, mr, bs, br, bms, bmr, rs, rr,
):
    y = lax.axis_index("group")
    s = lax.axis_index("shard")
    x, z, k = s // 8, (s // 2) % 4, s % 2
    here = (x, y, z)
    at = [[here[a] for a in order] for order in ORDERS]
    scale = 1.0 / math.sqrt(D)
    T3 = range(3)

    def device(c, core):
        return (c[1], (c[0] * 4 + c[2]) * 2 + core)

    def shifted(axis, r):
        c = list(here)
        c[axis] = (c[axis] + r) % 4
        return device(c, k)

    sibling = device(here, 1 - k)
    partner = [[shifted(axis, r) for r in (1, 2, 3)] for axis in range(3)]

    pending = []

    def remote(src, dst, ssem, rsem, target):
        pltpu.make_async_remote_copy(
            src_ref=src, dst_ref=dst, send_sem=ssem, recv_sem=rsem,
            device_id=target, device_id_type=MESH,
        ).start()
        pending.append((src, ssem))

    def arrived(dst, rsem):
        pltpu.make_async_remote_copy(
            src_ref=dst, dst_ref=dst, send_sem=rsem, recv_sem=rsem,
            device_id=sibling, device_id_type=MESH,
        ).wait_recv()

    barrier = pltpu.get_barrier_semaphore()
    for axis in range(3):
        for r in range(3):
            pl.semaphore_signal(barrier, inc=1, device_id=partner[axis][r], device_id_type=MESH)
    pl.semaphore_signal(barrier, inc=1, device_id=sibling, device_id_type=MESH)
    load = pltpu.make_async_copy(l_hbm, lab, sem_l)
    load.start()

    turned_meta = meta_ref[...].T
    for t in T3:
        gm[t, k, 0, 0, 0] = turned_meta[t * 16:(t + 1) * 16, :].astype(BF)
        gq[t, k, 0, 0, 0] = q_ref[:, t * 256:(t + 1) * 256]
    total[...] = jnp.zeros_like(total)
    pl.semaphore_wait(barrier, 10)

    UNITS = ((0, 0, (0, 1)), (1, 0, (0, 1)), (1, 0, (1, 3)), (2, 0, (0, 1)), (2, 0, (1, 3)), (2, 1, (0, 4)), (2, 2, (0, 4)), (2, 3, (0, 4)))

    def region(t, n, place):
        ring, j, (lo, size) = UNITS[n]
        if ring == 0:
            return gq.at[t, k, 0, 0, pl.ds(place, 1)]
        if ring == 1:
            return gq.at[t, k, 0, place, pl.ds(lo, size)]
        return gq.at[t, k, place, j, pl.ds(lo, size)]

    def half(ref, way):
        return ref.at[:, pl.ds(64 * way, 64)]

    def toward(t, n, way):
        return partner[ORDERS[t][UNITS[n][0]]][0 if way == 0 else 2]

    def both_ways(t, n):
        for way in (0, 1):
            remote(region(t, n, 0), region(t, n, 1 + way), qs.at[t, n, 0, way], qr.at[t, n, 0, way], toward(t, n, way))

    def onward(t, n, way):
        arrived(region(t, n, 1 + way), qr.at[t, n, 0, way])
        remote(
            half(region(t, n, 1 + way), way), half(region(t, n, 3), way),
            qs.at[t, n, 1, way], qr.at[t, n, 1, way], toward(t, n, way),
        )

    def far(t, n):
        for way in (0, 1):
            arrived(half(region(t, n, 3), way), qr.at[t, n, 1, way])

    def meta_region(t, ring, place):
        if ring == 0:
            return gm.at[t, k, 0, 0, place]
        if ring == 1:
            return gm.at[t, k, 0, place]
        return gm.at[t, k, place]

    def meta_send(ring):
        for t in T3:
            for r in (1, 2, 3):
                remote(
                    meta_region(t, ring, 0), meta_region(t, ring, PLACE[r]),
                    ms.at[t, ring, r - 1], mr.at[t, ring, r - 1], partner[ORDERS[t][ring]][r - 1],
                )

    def meta_wait(ring):
        for t in T3:
            for r in (1, 2, 3):
                arrived(meta_region(t, ring, PLACE[r]), mr.at[t, ring, r - 1])

    def to_sibling(t, r3, j):
        ref = gq.at[t, k, r3, j]
        remote(ref, ref, bs.at[t, r3, j], br.at[t, r3, j], sibling)

    def from_sibling(r3s, js):
        for t in T3:
            for r3 in r3s:
                for j in js:
                    arrived(gq.at[t, 1 - k, r3, j], br.at[t, r3, j])

    def meta_sibling(r3):
        for t in T3:
            ref = gm.at[t, k, r3]
            remote(ref, ref, bms.at[t, r3], bmr.at[t, r3], sibling)

    def prepare(c, _):
        here_l = pl.ds(pl.multiple_of(c * LBL, LBL), LBL)
        slab = lab[here_l, :]
        lp[here_l, :] = dot(slab, p_ref[...], 1, 1).astype(BF)
        lt[:, here_l] = slab.T
        return 0

    def prepare_some(lo, hi):
        lax.fori_loop(lo, hi, prepare, 0)

    number = y * 32 + s
    first = number * CL
    octave = first // 128
    base = (128 + first % 128).astype(F32)
    power = lax.shift_left(jnp.int32(1), octave.astype(jnp.int32)).astype(F32)

    def four_chips(group, step):
        words = []
        for h in range(4):
            word = 0
            for n in range(4):
                o = CHIPS[group * GROUP + h * 4 + n]
                word |= (o[0] + 4 * o[1] + 16 * o[2]) << (6 * n)
            words.append(word)
        word = jnp.where(step == 0, words[0], jnp.where(step == 1, words[1], jnp.where(step == 2, words[2], words[3])))
        places = []
        for n in range(4):
            code = (word // (1 << (6 * n))) % 64
            places.append((code % 4, (code // 4) % 4, code // 16))
        return places

    def pair(ref, c, t):
        a1, a2, a3 = ORDERS[t]
        return ref[t, 0, c[a3], c[a2], c[a1]], ref[t, 1, c[a3], c[a2], c[a1]]

    lane = lax.broadcasted_iota(jnp.int32, (16, 256), 1)
    sub = lax.broadcasted_iota(jnp.int32, (16, 256), 0)
    own_slot = jnp.where(sub // W == lane // QD, sub % W, -2).astype(F32)
    own_cluster = (
        lax.broadcasted_iota(jnp.int32, (CL, 128), 0) == lax.broadcasted_iota(jnp.int32, (CL, 128), 1) // 16
    )
    lane_chip = lax.broadcasted_iota(jnp.int32, (8, 128), 1) // 16
    before = lax.broadcasted_iota(jnp.int32, (256, 256), 0)
    after = lax.broadcasted_iota(jnp.int32, (256, 256), 1)
    tri = jnp.where((before < after) & (before // QD == after // QD), 1.0, 0.0).astype(BF)

    def pick(group):
        def names(step, _):
            for u, c in enumerate(four_chips(group, step)):
                a0, a1 = pair(gm, c, 0)
                b0, b1 = pair(gm, c, 1)
                ids = jnp.concatenate(
                    [jnp.concatenate([a0, b0], axis=0), jnp.concatenate([a1, b1], axis=0)], axis=1
                ).astype(F32)
                column = lax.broadcasted_iota(jnp.int32, (32, 256), 0).astype(F32) + 1.0
                found = []
                for n in range(CL):
                    found.append(jnp.sum(jnp.where(ids == (base + n) * power, column, 0.0), axis=0, keepdims=True))
                cp[pl.ds(pl.multiple_of(step * 4 * CL + u * CL, CL), CL), :] = jnp.concatenate(found, axis=0)
            return 0

        lax.fori_loop(0, GROUP // 4, names, 0)
        picked = cp[...] > 0.0
        rank = dot(jnp.where(picked, 1.0, 0.0).astype(BF), tri)
        cd[...] = jnp.where(picked, rank, -1.0)

        def hot(step, _):
            for u, c in enumerate(four_chips(group, step)):
                here_c = pl.ds(pl.multiple_of(step * 4 * CL + u * CL, CL), CL)
                code = cd[here_c, :]
                onehot = jnp.concatenate(
                    [jnp.where(code[n:n + 1, :] == own_slot, 1.0, 0.0).astype(BF) for n in range(CL)], axis=0
                )
                oh[group * GROUP + step * 4 + u] = onehot
                m0, m1 = pair(gm, c, 2)
                marks = jnp.concatenate([m0, m1], axis=1).astype(F32)
                column = cp[here_c, :]
                shifted_marks = jnp.concatenate(
                    [jnp.where(marks[n:n + 1, :] == column, marks[4 + n:5 + n, :], 0.0) for n in range(4)], axis=0
                ).astype(BF)
                spread = dot(shifted_marks, onehot, 1, 1)
                mk[step * 4 + u] = jnp.concatenate(
                    [
                        jnp.sum(jnp.where(own_cluster, spread[n * CL:(n + 1) * CL, :], 0.0), axis=0, keepdims=True)
                        for n in range(4)
                    ]
                    + [jnp.zeros((4, 128), F32)],
                    axis=0,
                )
            return 0

        lax.fori_loop(0, GROUP // 4, hot, 0)
        for h in range(GROUP // 8):
            for n in range(CL):
                line_marks = jnp.zeros((8, 128), F32)
                for i in range(8):
                    turned = pltpu.roll(mk[h * 8 + i], (16 * (i - n)) % 128, 1)
                    line_marks = jnp.where(lane_chip == i, turned, line_marks)
                mc[group, n, :, h * 128:(h + 1) * 128] = line_marks

    def gather_rows(group):
        def choose(step, _):
            for u, c in enumerate(four_chips(group, step)):
                onehot = oh[group * GROUP + step * 4 + u]
                at_row = pl.ds(pl.multiple_of(step * 64 + u * 16, 16), 16)
                for t in T3:
                    q0, q1 = pair(gq, c, t)
                    got = dot(onehot, jnp.concatenate([q0, q1], axis=0)).astype(BF)
                    for n in range(CL):
                        rows[n, at_row, t * 256:(t + 1) * 256] = got[n * 16:(n + 1) * 16, :]
            return 0

        lax.fori_loop(0, GROUP // 4, choose, 0)

    def sum_rows(group):
        def cluster(m0, _):
            ns = [2 * m0, 2 * m0 + 1]
            label = lax.broadcasted_iota(jnp.int32, (LBL, GROUP * 16), 0).astype(F32) + 1.0
            places = [pl.ds(pl.multiple_of(n * LBL, LBL), LBL) for n in ns]
            scores = [dot(lp[h, :], rows[n], 1, 1) * scale for n, h in zip(ns, places)]
            signals = []
            for n, score in zip(ns, scores):
                m = mc[group, n]
                hit = (m[0:1] == label) | (m[1:2] == label) | (m[2:3] == label) | (m[3:4] == label)
                signals.append((1.0 / (1.0 + jnp.exp(-score)) - jnp.where(hit, 1.0, 0.0)).astype(BF))
            for n, h, signal in zip(ns, places, signals):
                total[h, :] += dot(signal, rows[n])
            return 0

        lax.fori_loop(0, CL // 2, cluster, 0)

    def group_work(group):
        gather_rows(group)
        sum_rows(group)

    for t in T3:
        both_ways(t, 0)
    meta_send(0)
    for t in T3:
        both_ways(t, 1)
        both_ways(t, 3)
    for t in T3:
        for way in (0, 1):
            onward(t, 0, way)
    meta_wait(0)
    meta_send(1)
    for t in T3:
        far(t, 0)
        both_ways(t, 2)
        both_ways(t, 4)
        to_sibling(t, 0, 0)
    for t in T3:
        for way in (0, 1):
            onward(t, 1, way)
            onward(t, 3, way)
    load.wait()
    prepare_some(0, 1)
    meta_wait(1)
    meta_send(2)
    meta_sibling(0)
    prepare_some(1, 3)
    for way in (0, 1):
        for t in T3:
            onward(t, 2, way)
            both_ways(t, 5 + way)
            to_sibling(t, 0, 1 + way)
    meta_wait(2)
    for r3 in (1, 2, 3):
        meta_sibling(r3)
    prepare_some(3, 8)
    for t in T3:
        far(t, 1)
        far(t, 2)
        both_ways(t, 7)
        to_sibling(t, 0, 3)
    for t in T3:
        for way in (0, 1):
            onward(t, 4, way)
            to_sibling(t, 1 + way, 0)
    for t in T3:
        for r3 in range(4):
            arrived(gm.at[t, 1 - k, r3], bmr.at[t, r3])
    pick(0)
    pick(1)

    def lines_after(j):
        for t in T3:
            for way in (0, 1):
                onward(t, 4 + j, way)
                to_sibling(t, 1 + way, j)

    def far_after(ns, j):
        for t in T3:
            for n in ns:
                far(t, n)
            to_sibling(t, 3, j)

    lines_after(1)
    pick(2)
    far_after((3, 4), 0)
    pick(3)
    lines_after(2)
    from_sibling((0,), range(4))
    from_sibling((1, 2), (0, 1))
    from_sibling((3,), (0,))
    group_work(0)
    far_after((5,), 1)
    lines_after(3)
    from_sibling((1, 2), (2,))
    from_sibling((3,), (1,))
    group_work(1)
    far_after((6,), 2)
    from_sibling((1, 2), (3,))
    from_sibling((3,), (2,))
    group_work(2)
    far_after((7,), 3)
    from_sibling((3,), (3,))
    group_work(3)

    def halve(n, _):
        rows[n] = total[pl.ds(pl.multiple_of(n * LBL, LBL), LBL), :].astype(BF)
        return 0

    lax.fori_loop(0, CL, halve, 0)

    def project(which):
        at_half = pl.ds(pl.multiple_of(which * 384, 128), 384)
        for t in T3:
            for m in range(2):
                add = dot(lt[at_half, m * 1024:(m + 1) * 1024], rows[m * 4:(m + 1) * 4, :, t * 256:(t + 1) * 256].reshape(1024, 256))
                if m == 0:
                    pj[at_half, t * 256:(t + 1) * 256] = add
                else:
                    pj[at_half, t * 256:(t + 1) * 256] += add

    other_half = pl.ds(pl.multiple_of((1 - k) * 384, 128), 384)
    own_half = pl.ds(pl.multiple_of(k * 384, 128), 384)
    project(1 - k)
    remote(pj.at[other_half], rb0, rs.at[0], rr.at[0], sibling)
    project(k)

    eye = lax.broadcasted_iota(jnp.int32, (128, 128), 0) == lax.broadcasted_iota(jnp.int32, (128, 128), 1)

    def adagrad(n, _):
        here_l = pl.ds(pl.multiple_of(n * LBL, LBL), LBL)
        high, low = split(total[here_l, :])
        grad = (dot(high, p_ref[...]) + dot(low, p_ref[...])) * scale
        mean = jnp.sum(grad * grad, axis=1, keepdims=True) * (1.0 / D)
        old = jnp.concatenate(
            [
                jnp.sum(jnp.where(eye, acc_ref[pl.ds(n * 2 + h, 1), :], 0.0), axis=1, keepdims=True)
                for h in range(2)
            ],
            axis=0,
        )
        sums = old + mean
        for h in range(2):
            sums_ref[pl.ds(n * 2 + h, 1), :] = jnp.sum(
                jnp.where(eye, sums[h * 128:(h + 1) * 128], 0.0), axis=0, keepdims=True
            )
        rows[n] = (lab[here_l, :].astype(F32) - grad * (1.0 / jnp.sqrt(sums))).astype(BF)
        return 0

    def adagrad_some(lo, hi):
        lax.fori_loop(lo, hi, adagrad, 0)

    arrived(rb0, rr.at[0])
    mine_sum = pj[own_half, :] + rb0[...]
    sb[...] = mine_sum.astype(BF)

    def cols(t):
        return pl.ds(t * 256, 256)

    def exchange(n, t, ring, src_of, dst_of):
        for r in (1, 2, 3):
            slot = 1 + n * 9 + t * 3 + r - 1
            remote(src_of(r), dst_of(r), rs.at[slot], rr.at[slot], partner[ORDERS[t][ring]][r - 1])

    def exchanged(n, t, ring, dst_of):
        for r in (1, 2, 3):
            slot = 1 + n * 9 + t * 3 + r - 1
            arrived(dst_of(r, (at[t][ring] - r + 4) % 4), rr.at[slot])

    def piece(i):
        return pl.ds(pl.multiple_of(i * 96, 32), 96)

    def full_piece(i):
        return pl.ds(pl.multiple_of(k * 384 + i * 96, 32), 96)

    def quarter(i):
        return pl.ds(pl.multiple_of(i * 24, 8), 24)

    for t in T3:
        exchange(0, t, 0, lambda r: sb.at[piece((at[t][0] + r) % 4), cols(t)], lambda r: rb1.at[t, r - 1])
    adagrad_some(0, 2)
    for t in T3:
        exchanged(0, t, 0, lambda r, i: rb1.at[t, r - 1])
        s1[t] = (
            (sb[piece(at[t][0]), cols(t)].astype(F32) + rb1[t, 0].astype(F32))
            + (rb1[t, 1].astype(F32) + rb1[t, 2].astype(F32))
        )
        exchange(1, t, 1, lambda r: s1.at[t, quarter((at[t][1] + r) % 4)], lambda r: rb2.at[t, r - 1])
    adagrad_some(2, 3)
    for t in T3:
        exchanged(1, t, 1, lambda r, i: rb2.at[t, r - 1])
        s2[t] = s1[t, quarter(at[t][1])] + rb2[t, 0] + rb2[t, 1] + rb2[t, 2]
        rb3[t, at[t][2]] = s2[t]
        exchange(2, t, 2, lambda r: s2.at[t], lambda r: rb3.at[t, at[t][2]])
    adagrad_some(3, 4)
    for t in T3:
        exchanged(2, t, 2, lambda r, i: rb3.at[t, i])
        mine = quarter(at[t][1])
        g1[t, mine] = (rb3[t, 0] + rb3[t, 1]) + (rb3[t, 2] + rb3[t, 3])
        exchange(3, t, 1, lambda r: g1.at[t, mine], lambda r: g1.at[t, mine])
    adagrad_some(4, 5)
    for t in T3:
        exchanged(3, t, 1, lambda r, i: g1.at[t, quarter(i)])
        g1b[t] = g1[t].astype(BF)
        full[full_piece(at[t][0]), cols(t)] = g1b[t]
        exchange(4, t, 0, lambda r: g1b.at[t], lambda r: full.at[full_piece(at[t][0]), cols(t)])
    adagrad_some(5, 7)
    for t in T3:
        exchanged(4, t, 0, lambda r, i: full.at[full_piece(i), cols(t)])
    remote(full.at[own_half], full.at[own_half], rs.at[46], rr.at[46], sibling)
    adagrad_some(7, 8)
    store = pltpu.make_async_copy(rows, new_hbm, sem_o)
    store.start()
    arrived(full.at[other_half], rr.at[46])

    proj_ref[...] = full[...]
    wide = full[...].astype(F32)
    squares = jnp.sum(wide * wide) * (scale * scale)
    factor = jnp.minimum(1.0, D / jnp.sqrt(squares + 1e-06)) * scale
    factor_ref[...] = jnp.full((8, 128), 1.0, F32) * factor

    store.wait()
    for src, ssem in pending:
        pltpu.make_async_remote_copy(
            src_ref=src, dst_ref=src, send_sem=ssem, recv_sem=ssem,
            device_id=sibling, device_id_type=MESH,
        ).wait_send()


def on_device(queries, projection, labels, accumulator, shortlist, positives):
    ids = shortlist.astype(jnp.int32)
    codes = lax.shift_left(128 + (ids & 127), lax.shift_right_logical(ids, 7))
    marks = jnp.concatenate([lax.shift_right_logical(positives, 8) + 1, (positives & 255) + 1], axis=1)
    meta = jnp.concatenate([codes, marks, jnp.zeros((QD, 88), jnp.int32)], axis=1).astype(F32)
    vmem = pl.BlockSpec(memory_space=pltpu.VMEM)
    hbm = pl.BlockSpec(memory_space=pl.ANY)
    dma = pltpu.SemaphoreType.DMA
    new_labels, sums, proj, factor = pl.pallas_call(
        kernel,
        out_shape=(
            jax.ShapeDtypeStruct((CL, LBL, D), BF),
            jax.ShapeDtypeStruct((16, 128), F32),
            jax.ShapeDtypeStruct((D, D), BF),
            jax.ShapeDtypeStruct((8, 128), F32),
        ),
        in_specs=[vmem] * 4 + [hbm],
        out_specs=(hbm, vmem, vmem, vmem),
        scratch_shapes=[
            pltpu.VMEM((3, 2, 4, 4, 4, QD, 256), BF),
            pltpu.VMEM((3, 2, 4, 4, 4, 16, QD), BF),
            pltpu.VMEM((CL * LBL, D), BF),
            pltpu.VMEM((CL * LBL, D), BF),
            pltpu.VMEM((D, CL * LBL), BF),
            pltpu.VMEM((CL * LBL, D), F32),
            pltpu.VMEM((CL, GROUP * 16, D), BF),
            pltpu.VMEM((GROUP * CL, 256), F32),
            pltpu.VMEM((GROUP * CL, 256), F32),
            pltpu.VMEM((64, 128, 256), BF),
            pltpu.VMEM((GROUP, 8, 128), F32),
            pltpu.VMEM((GROUPS, CL, 8, GROUP * 16), F32),
            pltpu.VMEM((D, D), F32),
            pltpu.VMEM((384, D), F32),
            pltpu.VMEM((384, D), BF),
            pltpu.VMEM((3, 3, 96, 256), BF),
            pltpu.VMEM((3, 3, 24, 256), F32),
            pltpu.VMEM((3, 4, 24, 256), F32),
            pltpu.VMEM((3, 96, 256), F32),
            pltpu.VMEM((3, 24, 256), F32),
            pltpu.VMEM((3, 96, 256), F32),
            pltpu.VMEM((3, 96, 256), BF),
            pltpu.VMEM((D, D), BF),
            dma, dma,
            dma((3, 8, 2, 2)), dma((3, 8, 2, 2)),
            dma((3, 3, 3)), dma((3, 3, 3)),
            dma((3, 4, 4)), dma((3, 4, 4)),
            dma((3, 4)), dma((3, 4)),
            dma((47,)), dma((47,)),
        ],
        compiler_params=pltpu.CompilerParams(
            collective_id=0, has_side_effects=True, vmem_limit_bytes=63 * 1024 * 1024
        ),
        cost_estimate=pl.CostEstimate(flops=20 * 10**9, bytes_accessed=20 * 10**6, transcendentals=0),
    )(queries, meta, projection, accumulator.reshape(16, 128), labels)
    proj_grad = proj.T.astype(F32) * factor[0, 0]
    return new_labels.reshape(CL * LBL, D), sums.reshape(-1), proj_grad


def solution(mesh):
    in_specs = (
        P(("group", "shard"), None),
        P(),
        P(("group", "shard"), None),
        P(("group", "shard")),
        P(("group", "shard"), None),
        P(("group", "shard"), None),
    )
    out_specs = (P(("group", "shard"), None), P(("group", "shard")), P())
    return jax.shard_map(
        on_device, mesh=mesh, in_specs=in_specs, out_specs=out_specs, check_vma=False
    )
```

```python
import functools
import math

import jax
import jax.numpy as jnp
from jax import lax
from jax.experimental import pallas as pl
from jax.experimental.pallas import tpu as pltpu
from jax.sharding import PartitionSpec as P

MESH = pl.DeviceIdType.MESH
LBL = 256
QD = 128
D = 768
CL = 8
W = 8
BF = jnp.bfloat16
F32 = jnp.float32
ORDERS = ((0, 1, 2), (1, 2, 0), (2, 0, 1))
PLACE = {1: 1, 2: 3, 3: 2}
GROUP = 16
GROUPS = 4


def arrival(place):
    worst = 0
    for order in ORDERS:
        third, second = place[order[2]], place[order[1]]
        tick = ((0, 0, 0, 0), (1, 2, 4, 6), (1, 2, 4, 6), (3, 5, 7, 8))[third][second]
        worst = max(worst, tick)
    return worst


CHIPS = sorted(
    [(a, b, c) for a in range(4) for b in range(4) for c in range(4)],
    key=lambda o: (arrival(o), o),
)


def dot(a, b, ca=1, cb=0):
    return lax.dot_general(a, b, (((ca,), (cb,)), ((), ())), preferred_element_type=F32)


def split(value):
    high = value.astype(BF)
    return high, (value - high.astype(F32)).astype(BF)


def kernel(
    q_ref, list_ref, pos_ref, p_ref, acc_ref, l_hbm,
    new_hbm, sums_ref, full_hbm,
    gq, gm, lab, lp, lt, total, rows, cp, cd, oh, mk, mc, pj, rb0, sb, rb1, rb2, rb3, s1, s2, g1, full,
    sem_l, sem_o, sem_f,
    qs, qr, ms, mr, bs, br, bms, bmr, rs, rr,
):
    y = lax.axis_index("group")
    s = lax.axis_index("shard")
    x, z, k = s // 8, (s // 2) % 4, s % 2
    here = (x, y, z)
    at = [[here[a] for a in order] for order in ORDERS]
    scale = 1.0 / math.sqrt(D)
    T3 = range(3)

    def device(c, core):
        return (c[1], (c[0] * 4 + c[2]) * 2 + core)

    def shifted(axis, r):
        c = list(here)
        c[axis] = (c[axis] + r) % 4
        return device(c, k)

    sibling = device(here, 1 - k)
    partner = [[shifted(axis, r) for r in (1, 2, 3)] for axis in range(3)]

    pending = []

    def remote(src, dst, ssem, rsem, target):
        pltpu.make_async_remote_copy(
            src_ref=src, dst_ref=dst, send_sem=ssem, recv_sem=rsem,
            device_id=target, device_id_type=MESH,
        ).start()
        pending.append((src, ssem))

    def arrived(dst, rsem):
        pltpu.make_async_remote_copy(
            src_ref=dst, dst_ref=dst, send_sem=rsem, recv_sem=rsem,
            device_id=sibling, device_id_type=MESH,
        ).wait_recv()

    def drain():
        for src, ssem in pending:
            pltpu.make_async_remote_copy(
                src_ref=src, dst_ref=src, send_sem=ssem, recv_sem=ssem,
                device_id=sibling, device_id_type=MESH,
            ).wait_send()
        pending.clear()

    barrier = pltpu.get_barrier_semaphore()
    for axis in range(3):
        for r in range(3):
            pl.semaphore_signal(barrier, inc=1, device_id=partner[axis][r], device_id_type=MESH)
    pl.semaphore_signal(barrier, inc=1, device_id=sibling, device_id_type=MESH)
    load = pltpu.make_async_copy(l_hbm, lab, sem_l)
    load.start()

    ids = list_ref[...]
    pos = pos_ref[...]

    codes = lax.shift_left(128 + (ids & 127), lax.shift_right_logical(ids, 7)).astype(F32)
    marks = jnp.concatenate(
        [
            (lax.shift_right_logical(pos, 8) + 1).astype(F32),
            ((pos & 255) + 1).astype(F32),
            jnp.zeros((8, QD), F32),
        ],
        axis=0,
    )
    for t, value in enumerate((codes[:16], codes[16:], marks)):
        gm[t, k, 0, 0, 0] = value.astype(BF)
    for t in T3:
        gq[t, k, 0, 0, 0] = q_ref[:, t * 256:(t + 1) * 256]
    total[...] = jnp.zeros_like(total)
    pl.semaphore_wait(barrier, 10)

    UNITS = (
        (0, 0, (0, 1)),
        (1, 0, (0, 1)), (1, 0, (1, 2)), (1, 0, (3, 1)),
        (2, 0, (0, 1)), (2, 0, (1, 2)), (2, 0, (3, 1)),
        (2, 1, (0, 4)), (2, 2, (0, 4)), (2, 3, (0, 4)),
    )

    def region(t, n, place):
        ring, j, (lo, size) = UNITS[n]
        if ring == 0:
            return gq.at[t, k, 0, 0, pl.ds(place, 1)]
        if ring == 1:
            return gq.at[t, k, 0, place, pl.ds(lo, size)]
        return gq.at[t, k, place, j, pl.ds(lo, size)]

    def half(ref, way):
        return ref.at[:, pl.ds(64 * way, 64)]

    def toward(t, n, way):
        return partner[ORDERS[t][UNITS[n][0]]][0 if way == 0 else 2]

    def both_ways(t, n):
        for way in (0, 1):
            remote(region(t, n, 0), region(t, n, 1 + way), qs.at[t, n, 0, way], qr.at[t, n, 0, way], toward(t, n, way))

    def onward(t, n, way):
        arrived(region(t, n, 1 + way), qr.at[t, n, 0, way])
        remote(
            half(region(t, n, 1 + way), way), half(region(t, n, 3), way),
            qs.at[t, n, 1, way], qr.at[t, n, 1, way], toward(t, n, way),
        )

    def far(t, n):
        for way in (0, 1):
            arrived(half(region(t, n, 3), way), qr.at[t, n, 1, way])

    def meta_region(t, ring, place):
        if ring == 0:
            return gm.at[t, k, 0, 0, place]
        if ring == 1:
            return gm.at[t, k, 0, place]
        return gm.at[t, k, place]

    def meta_send(ring):
        for t in T3:
            for r in (1, 2, 3):
                remote(
                    meta_region(t, ring, 0), meta_region(t, ring, PLACE[r]),
                    ms.at[t, ring, r - 1], mr.at[t, ring, r - 1], partner[ORDERS[t][ring]][r - 1],
                )

    def meta_wait(ring):
        for t in T3:
            for r in (1, 2, 3):
                arrived(meta_region(t, ring, PLACE[r]), mr.at[t, ring, r - 1])

    landed, shared = set(), set()

    def to_sibling(t, r3, j):
        ref = gq.at[t, k, r3, j]
        remote(ref, ref, bs.at[t, r3, j], br.at[t, r3, j], sibling)
        landed.add((t, r3, j))

    def require(group):
        lines = set()
        for o in CHIPS[group * GROUP:(group + 1) * GROUP]:
            for t in T3:
                lines.add((t, o[ORDERS[t][2]], o[ORDERS[t][1]]))
        assert lines <= landed
        for t, r3, j in sorted(lines - shared):
            arrived(gq.at[t, 1 - k, r3, j], br.at[t, r3, j])
        shared.update(lines)

    def meta_sibling(r3):
        for t in T3:
            ref = gm.at[t, k, r3]
            remote(ref, ref, bms.at[t, r3], bmr.at[t, r3], sibling)

    def prepare(c, _):
        here_l = pl.ds(pl.multiple_of(c * LBL, LBL), LBL)
        slab = lab[here_l, :]
        lp[here_l, :] = dot(slab, p_ref[...], 1, 1).astype(BF)
        lt[:, here_l] = slab.T
        return 0

    def prepare_some(lo, hi):
        lax.fori_loop(lo, hi, prepare, 0)

    number = y * 32 + s
    first = number * CL
    octave = first // 128
    base = (128 + first % 128).astype(F32)
    power = lax.shift_left(jnp.int32(1), octave.astype(jnp.int32)).astype(F32)

    def four_chips(group, step):
        words = []
        for h in range(4):
            word = 0
            for n in range(4):
                o = CHIPS[group * GROUP + h * 4 + n]
                word |= (o[0] + 4 * o[1] + 16 * o[2]) << (6 * n)
            words.append(word)
        word = jnp.where(step == 0, words[0], jnp.where(step == 1, words[1], jnp.where(step == 2, words[2], words[3])))
        places = []
        for n in range(4):
            code = (word // (1 << (6 * n))) % 64
            places.append((code % 4, (code // 4) % 4, code // 16))
        return places

    def pair(ref, c, t):
        a1, a2, a3 = ORDERS[t]
        return ref[t, 0, c[a3], c[a2], c[a1]], ref[t, 1, c[a3], c[a2], c[a1]]

    lane = lax.broadcasted_iota(jnp.int32, (16, 256), 1)
    sub = lax.broadcasted_iota(jnp.int32, (16, 256), 0)
    own_slot = jnp.where(sub // W == lane // QD, sub % W, -2).astype(F32)
    own_cluster = (
        lax.broadcasted_iota(jnp.int32, (CL, 128), 0) == lax.broadcasted_iota(jnp.int32, (CL, 128), 1) // 16
    )
    lane_chip = lax.broadcasted_iota(jnp.int32, (8, 128), 1) // 16
    before = lax.broadcasted_iota(jnp.int32, (256, 256), 0)
    after = lax.broadcasted_iota(jnp.int32, (256, 256), 1)
    tri = jnp.where((before < after) & (before // QD == after // QD), 1.0, 0.0).astype(BF)

    def pick(group):
        def names(step, _):
            for u, c in enumerate(four_chips(group, step)):
                a0, a1 = pair(gm, c, 0)
                b0, b1 = pair(gm, c, 1)
                ids = jnp.concatenate(
                    [jnp.concatenate([a0, b0], axis=0), jnp.concatenate([a1, b1], axis=0)], axis=1
                ).astype(F32)
                column = lax.broadcasted_iota(jnp.int32, (32, 256), 0).astype(F32) + 1.0
                found = []
                for n in range(CL):
                    found.append(jnp.sum(jnp.where(ids == (base + n) * power, column, 0.0), axis=0, keepdims=True))
                cp[pl.ds(pl.multiple_of(step * 4 * CL + u * CL, CL), CL), :] = jnp.concatenate(found, axis=0)
            return 0

        lax.fori_loop(0, GROUP // 4, names, 0)
        picked = cp[...] > 0.0
        rank = dot(jnp.where(picked, 1.0, 0.0).astype(BF), tri)
        cd[...] = jnp.where(picked, rank, -1.0)

        def hot(step, _):
            for u, c in enumerate(four_chips(group, step)):
                here_c = pl.ds(pl.multiple_of(step * 4 * CL + u * CL, CL), CL)
                code = cd[here_c, :]
                onehot = jnp.concatenate(
                    [jnp.where(code[n:n + 1, :] == own_slot, 1.0, 0.0).astype(BF) for n in range(CL)], axis=0
                )
                oh[group * GROUP + step * 4 + u] = onehot
                m0, m1 = pair(gm, c, 2)
                marks = jnp.concatenate([m0, m1], axis=1).astype(F32)
                column = cp[here_c, :]
                shifted_marks = jnp.concatenate(
                    [jnp.where(marks[n:n + 1, :] == column, marks[4 + n:5 + n, :], 0.0) for n in range(4)], axis=0
                ).astype(BF)
                spread = dot(shifted_marks, onehot, 1, 1)
                mk[step * 4 + u] = jnp.concatenate(
                    [
                        jnp.sum(jnp.where(own_cluster, spread[n * CL:(n + 1) * CL, :], 0.0), axis=0, keepdims=True)
                        for n in range(4)
                    ]
                    + [jnp.zeros((4, 128), F32)],
                    axis=0,
                )
            return 0

        lax.fori_loop(0, GROUP // 4, hot, 0)
        for h in range(GROUP // 8):
            for n in range(CL):
                line_marks = jnp.zeros((8, 128), F32)
                for i in range(8):
                    turned = pltpu.roll(mk[h * 8 + i], (16 * (i - n)) % 128, 1)
                    line_marks = jnp.where(lane_chip == i, turned, line_marks)
                mc[group, n, :, h * 128:(h + 1) * 128] = line_marks

    def gather_rows(group):
        def choose(step, _):
            for u, c in enumerate(four_chips(group, step)):
                onehot = oh[group * GROUP + step * 4 + u]
                at_row = pl.ds(pl.multiple_of(step * 64 + u * 16, 16), 16)
                for t in T3:
                    q0, q1 = pair(gq, c, t)
                    got = dot(onehot, jnp.concatenate([q0, q1], axis=0)).astype(BF)
                    for n in range(CL):
                        rows[n, at_row, t * 256:(t + 1) * 256] = got[n * 16:(n + 1) * 16, :]
            return 0

        lax.fori_loop(0, GROUP // 4, choose, 0)

    def sum_rows(group):
        def cluster(m0, _):
            label = lax.broadcasted_iota(jnp.int32, (LBL, GROUP * 16), 0).astype(F32) + 1.0

            def place(u):
                return pl.ds(pl.multiple_of((4 * m0 + u) * LBL, LBL), LBL)

            def scored(u):
                return dot(lp[place(u), :], rows[4 * m0 + u], 1, 1) * scale

            def signal(u, sc):
                m = mc[group, 4 * m0 + u]
                hit = (m[0:1] == label) | (m[1:2] == label) | (m[2:3] == label) | (m[3:4] == label)
                return (1.0 / (1.0 + jnp.exp(-sc)) - jnp.where(hit, 1.0, 0.0)).astype(BF)

            scores, signals = [scored(0), scored(1)], []
            for u in range(4):
                signals.append(signal(u, scores[u]))
                if u + 2 < 4:
                    scores.append(scored(u + 2))
                if u > 0:
                    total[place(u - 1), :] += dot(signals[u - 1], rows[4 * m0 + u - 1])
            total[place(3), :] += dot(signals[3], rows[4 * m0 + 3])
            return 0

        lax.fori_loop(0, CL // 4, cluster, 0)

    def group_work(group):
        gather_rows(group)
        sum_rows(group)

    def every(n, act):
        for t in T3:
            for way in (0, 1):
                act(t, n, way)

    def sharing(n, j):
        for t in T3:
            for way in (0, 1):
                onward(t, n, way)
                to_sibling(t, 1 + way, j)

    def far_after(ns, j, r3=3):
        for t in T3:
            for n in ns:
                far(t, n)
            to_sibling(t, r3, j)

    meta_send(0)
    for n in (0, 1, 4):
        for t in T3:
            both_ways(t, n)
    load.wait()
    prepare_some(0, 2)
    meta_wait(0)
    meta_send(1)
    for t in T3:
        for way in (0, 1):
            onward(t, 0, way)
        both_ways(t, 2)
    every(1, onward)
    every(4, onward)
    prepare_some(2, 4)
    meta_wait(1)
    meta_send(2)
    meta_sibling(0)
    for t in T3:
        far(t, 0)
        both_ways(t, 5)
        both_ways(t, 3)
        both_ways(t, 6)
        to_sibling(t, 0, 0)
    prepare_some(4, 8)
    every(2, onward)
    for t in T3:
        for way in (0, 1):
            onward(t, 3, way)
            to_sibling(t, 0, 1 + way)
        both_ways(t, 7)
    meta_wait(2)
    for r3 in (1, 2, 3):
        meta_sibling(r3)
    every(5, onward)
    for t in T3:
        for way in (0, 1):
            onward(t, 6, way)
            to_sibling(t, 1 + way, 0)
        both_ways(t, 8)
    for t in T3:
        for r3 in range(4):
            arrived(gm.at[t, 1 - k, r3], bmr.at[t, r3])
    pick(0)
    far_after((1, 2, 3), 3, 0)
    pick(1)
    for t in T3:
        for way in (0, 1):
            onward(t, 7, way)
            to_sibling(t, 1 + way, 1)
        both_ways(t, 9)
    pick(2)
    far_after((4, 5, 6), 0)
    require(0)
    gather_rows(0)
    sum_rows(0)
    sharing(8, 2)
    pick(3)
    far_after((7,), 1)
    require(1)
    gather_rows(1)
    sum_rows(1)
    sharing(9, 3)
    far_after((8,), 2)
    require(2)
    gather_rows(2)
    far_after((9,), 3)
    sum_rows(2)
    require(3)
    gather_rows(3)
    sum_rows(3)
    for t in T3:
        for r3 in range(4):
            for j in range(4):
                if (t, r3, j) not in shared:
                    arrived(gq.at[t, 1 - k, r3, j], br.at[t, r3, j])

    def halve(n, _):
        rows[n] = total[pl.ds(pl.multiple_of(n * LBL, LBL), LBL), :].astype(BF)
        return 0

    lax.fori_loop(0, CL, halve, 0)

    def project(which):
        at_half = pl.ds(pl.multiple_of(which * 384, 128), 384)
        for t in T3:
            for m in range(2):
                add = dot(lt[at_half, m * 1024:(m + 1) * 1024], rows[m * 4:(m + 1) * 4, :, t * 256:(t + 1) * 256].reshape(1024, 256))
                if m == 0:
                    pj[at_half, t * 256:(t + 1) * 256] = add
                else:
                    pj[at_half, t * 256:(t + 1) * 256] += add

    other_half = pl.ds(pl.multiple_of((1 - k) * 384, 128), 384)
    own_half = pl.ds(pl.multiple_of(k * 384, 128), 384)
    project(1 - k)
    remote(pj.at[other_half], rb0, rs.at[0], rr.at[0], sibling)
    project(k)

    eye = lax.broadcasted_iota(jnp.int32, (128, 128), 0) == lax.broadcasted_iota(jnp.int32, (128, 128), 1)

    def adagrad(n, _):
        here_l = pl.ds(pl.multiple_of(n * LBL, LBL), LBL)
        high, low = split(total[here_l, :])
        grad = (dot(high, p_ref[...]) + dot(low, p_ref[...])) * scale
        mean = jnp.sum(grad * grad, axis=1, keepdims=True) * (1.0 / D)
        old = jnp.concatenate(
            [
                jnp.sum(jnp.where(eye, acc_ref[pl.ds(n * 2 + h, 1), :], 0.0), axis=1, keepdims=True)
                for h in range(2)
            ],
            axis=0,
        )
        sums = old + mean
        for h in range(2):
            sums_ref[pl.ds(n * 2 + h, 1), :] = jnp.sum(
                jnp.where(eye, sums[h * 128:(h + 1) * 128], 0.0), axis=0, keepdims=True
            )
        rows[n] = (lab[here_l, :].astype(F32) - grad * (1.0 / jnp.sqrt(sums))).astype(BF)
        pltpu.make_async_copy(rows.at[n], new_hbm.at[here_l], sem_o.at[n]).start()
        return 0

    def adagrad_some(lo, hi):
        lax.fori_loop(lo, hi, adagrad, 0)

    arrived(rb0, rr.at[0])
    mine_sum = pj[own_half, :] + rb0[...]
    sb[...] = mine_sum.astype(BF)

    def cols(t):
        return pl.ds(t * 256, 256)

    def exchange(n, t, ring, src_of, dst_of):
        for r in (1, 2, 3):
            slot = 1 + n * 9 + t * 3 + r - 1
            remote(src_of(r), dst_of(r), rs.at[slot], rr.at[slot], partner[ORDERS[t][ring]][r - 1])

    def exchanged(n, t, ring, dst_of):
        for r in (1, 2, 3):
            slot = 1 + n * 9 + t * 3 + r - 1
            arrived(dst_of(r, (at[t][ring] - r + 4) % 4), rr.at[slot])

    def piece(i):
        return pl.ds(pl.multiple_of(i * 96, 32), 96)

    def full_piece(i):
        return pl.ds(pl.multiple_of(k * 384 + i * 96, 32), 96)

    def tiles(i):
        return pl.ds(i * 3, 3)

    def laid(r, l):
        return r * 2 + l, slice(r * 16, (r + 1) * 16), slice(l * 128, (l + 1) * 128)

    TILES = [laid(r, l) for r in range(6) for l in range(2)]

    for t in T3:
        exchange(0, t, 0, lambda r: sb.at[piece((at[t][0] + r) % 4), cols(t)], lambda r: rb1.at[t, r - 1])
    adagrad_some(0, 2)
    drain()
    for t in T3:
        exchanged(0, t, 0, lambda r, i: rb1.at[t, r - 1])
        summed = (
            (sb[piece(at[t][0]), cols(t)].astype(F32) + rb1[t, 0].astype(F32))
            + (rb1[t, 1].astype(F32) + rb1[t, 2].astype(F32))
        ).astype(BF)
        for n, down, across in TILES:
            s1[t, n] = summed[down, across]
        exchange(1, t, 1, lambda r: s1.at[t, tiles((at[t][1] + r) % 4)], lambda r: rb2.at[t, r - 1])
    adagrad_some(2, 3)
    for t in T3:
        exchanged(1, t, 1, lambda r, i: rb2.at[t, r - 1])
        s2[t] = (
            (s1[t, tiles(at[t][1])].astype(F32) + rb2[t, 0].astype(F32))
            + (rb2[t, 1].astype(F32) + rb2[t, 2].astype(F32))
        ).astype(BF)
        rb3[t, at[t][2]] = s2[t]
        exchange(2, t, 2, lambda r: s2.at[t], lambda r: rb3.at[t, at[t][2]])
    adagrad_some(3, 4)
    for t in T3:
        exchanged(2, t, 2, lambda r, i: rb3.at[t, i])
        mine = tiles(at[t][1])
        g1[t, mine] = (
            (rb3[t, 0].astype(F32) + rb3[t, 1].astype(F32)) + (rb3[t, 2].astype(F32) + rb3[t, 3].astype(F32))
        ).astype(BF)
        exchange(3, t, 1, lambda r: g1.at[t, mine], lambda r: g1.at[t, mine])
    adagrad_some(4, 5)

    def share_piece(t, r):
        ref = full.at[full_piece((at[t][0] - r + 4) % 4), cols(t)]
        remote(ref, ref, rs.at[46 + t * 4 + r], rr.at[46 + t * 4 + r], sibling)

    for t in T3:
        exchanged(3, t, 1, lambda r, i: g1.at[t, tiles(i)])
        summed = jnp.concatenate(
            [jnp.concatenate([g1[t, 2 * r], g1[t, 2 * r + 1]], axis=1) for r in range(6)], axis=0
        )
        mine = full.at[full_piece(at[t][0]), cols(t)]
        mine[...] = summed
        exchange(4, t, 0, lambda r: mine, lambda r: mine)
        share_piece(t, 0)
    adagrad_some(5, 7)
    for r in (1, 3, 2):
        for t in T3:
            slot = 1 + 4 * 9 + t * 3 + r - 1
            arrived(full.at[full_piece((at[t][0] - r + 4) % 4), cols(t)], rr.at[slot])
            share_piece(t, r)
    adagrad_some(7, 8)
    for t in T3:
        for r in range(4):
            i = (at[t][0] - r + 4) % 4
            arrived(full.at[pl.ds(pl.multiple_of((1 - k) * 384 + i * 96, 32), 96), cols(t)], rr.at[46 + t * 4 + r])
    out = pltpu.make_async_copy(full, full_hbm, sem_f)
    out.start()
    for n in range(CL):
        pltpu.make_async_copy(rows.at[n], new_hbm.at[pl.ds(n * LBL, LBL)], sem_o.at[n]).wait()
    drain()
    out.wait()


def finish(new_hbm, sums_ref, full_hbm, labels_hbm, acc_ref, grad_hbm, held, full, grad, sem_in, sem_out, sem_f, sem_g):
    parts = [pl.ds(n * LBL, LBL) for n in range(CL)]
    bands = [pl.ds(n * 128, 128) for n in range(D // 128)]
    loads = [pltpu.make_async_copy(full_hbm.at[b], full.at[b], sem_f.at[n]) for n, b in enumerate(bands)]
    stores = [pltpu.make_async_copy(grad.at[b], grad_hbm.at[b], sem_g.at[n]) for n, b in enumerate(bands)]
    ins = [pltpu.make_async_copy(new_hbm.at[p], held.at[p], sem_in.at[n]) for n, p in enumerate(parts)]
    outs = [pltpu.make_async_copy(held.at[p], labels_hbm.at[p], sem_out.at[n]) for n, p in enumerate(parts)]
    for copy in loads + ins:
        copy.start()
    acc_ref[...] = sums_ref[...]
    scale = 1.0 / math.sqrt(D)
    squares = jnp.zeros((8, D), F32)
    for n, b in enumerate(bands):
        loads[n].wait()
        wide = full[b, :].astype(F32)
        squares = squares + jnp.sum((wide * wide).reshape(16, 8, D), axis=0)
    for n in range(CL):
        ins[n].wait()
        outs[n].start()
    squares = jnp.sum(squares, keepdims=True) * (scale * scale)
    factor = jnp.minimum(1.0, D / jnp.sqrt(squares + 1e-06)) * scale
    for n, b in enumerate(bands):
        grad[b, :] = full[:, n * 128:(n + 1) * 128].astype(F32).T * factor
        stores[n].start()
    for copy in outs + stores:
        copy.wait()


def on_device(queries, projection, labels, accumulator, shortlist, positives):
    vmem = pl.BlockSpec(memory_space=pltpu.VMEM)
    hbm = pl.BlockSpec(memory_space=pl.ANY)
    dma = pltpu.SemaphoreType.DMA
    new_labels, sums, proj = pl.pallas_call(
        kernel,
        out_shape=(
            jax.ShapeDtypeStruct((CL * LBL, D), BF),
            jax.ShapeDtypeStruct((16, 128), F32),
            jax.ShapeDtypeStruct((D, D), BF),
        ),
        in_specs=[vmem] * 5 + [hbm],
        out_specs=(hbm, vmem, hbm),
        scratch_shapes=[
            pltpu.VMEM((3, 2, 4, 4, 4, QD, 256), BF),
            pltpu.VMEM((3, 2, 4, 4, 4, 16, QD), BF),
            pltpu.VMEM((CL * LBL, D), BF),
            pltpu.VMEM((CL * LBL, D), BF),
            pltpu.VMEM((D, CL * LBL), BF),
            pltpu.VMEM((CL * LBL, D), F32),
            pltpu.VMEM((CL, GROUP * 16, D), BF),
            pltpu.VMEM((GROUP * CL, 256), F32),
            pltpu.VMEM((GROUP * CL, 256), F32),
            pltpu.VMEM((64, 128, 256), BF),
            pltpu.VMEM((GROUP, 8, 128), F32),
            pltpu.VMEM((GROUPS, CL, 8, GROUP * 16), F32),
            pltpu.VMEM((D, D), F32),
            pltpu.VMEM((384, D), F32),
            pltpu.VMEM((384, D), BF),
            pltpu.VMEM((3, 3, 96, 256), BF),
            pltpu.VMEM((3, 3, 3, 16, 128), BF),
            pltpu.VMEM((3, 4, 3, 16, 128), BF),
            pltpu.VMEM((3, 12, 16, 128), BF),
            pltpu.VMEM((3, 3, 16, 128), BF),
            pltpu.VMEM((3, 12, 16, 128), BF),
            pltpu.VMEM((D, D), BF),
            dma, dma((CL,)), dma,
            dma((3, 10, 2, 2)), dma((3, 10, 2, 2)),
            dma((3, 3, 3)), dma((3, 3, 3)),
            dma((3, 4, 4)), dma((3, 4, 4)),
            dma((3, 4)), dma((3, 4)),
            dma((58,)), dma((58,)),
        ],
        compiler_params=pltpu.CompilerParams(
            collective_id=0, has_side_effects=True, vmem_limit_bytes=63 * 1024 * 1024
        ),
        cost_estimate=pl.CostEstimate(flops=20 * 10**9, bytes_accessed=20 * 10**6, transcendentals=0),
    )(queries, shortlist.T, positives.T, projection, accumulator.reshape(16, 128), labels)
    labels_out, sums_out, grad = pl.pallas_call(
        finish,
        out_shape=(
            jax.ShapeDtypeStruct((CL * LBL, D), BF),
            jax.ShapeDtypeStruct((16, 128), F32),
            jax.ShapeDtypeStruct((D, D), F32),
        ),
        in_specs=[hbm, vmem, hbm],
        out_specs=(hbm, vmem, hbm),
        scratch_shapes=[
            pltpu.VMEM((CL * LBL, D), BF),
            pltpu.VMEM((D, D), BF),
            pltpu.VMEM((D, D), F32),
            dma((CL,)), dma((CL,)), dma((D // 128,)), dma((D // 128,)),
        ],
        compiler_params=pltpu.CompilerParams(vmem_limit_bytes=63 * 1024 * 1024),
    )(new_labels, sums, proj)
    return labels_out, sums_out.reshape(-1), grad


def solution(mesh):
    in_specs = (
        P(("group", "shard"), None),
        P(),
        P(("group", "shard"), None),
        P(("group", "shard")),
        P(("group", "shard"), None),
        P(("group", "shard"), None),
    )
    out_specs = (P(("group", "shard"), None), P(("group", "shard")), P())
    return jax.shard_map(
        on_device, mesh=mesh, in_specs=in_specs, out_specs=out_specs, check_vma=False
    )
```

```python
import functools
import math

import jax
import jax.numpy as jnp
from jax import lax
from jax.experimental import pallas as pl
from jax.experimental.pallas import tpu as pltpu
from jax.sharding import PartitionSpec as P

MESH = pl.DeviceIdType.MESH
LBL = 256
QD = 128
D = 768
CL = 8
W = 8
BF = jnp.bfloat16
F32 = jnp.float32
ORDERS = ((0, 1, 2), (1, 2, 0), (2, 0, 1))
PLACE = {1: 1, 2: 3, 3: 2}
GROUP = 16
GROUPS = 4


def arrival(place):
    worst = 0
    for order in ORDERS:
        third, second = place[order[2]], place[order[1]]
        tick = ((0, 0, 0, 0), (1, 2, 4, 6), (1, 2, 4, 6), (3, 5, 7, 8))[third][second]
        worst = max(worst, tick)
    return worst


CHIPS = sorted(
    [(a, b, c) for a in range(4) for b in range(4) for c in range(4)],
    key=lambda o: (arrival(o), o),
)


def dot(a, b, ca=1, cb=0):
    return lax.dot_general(a, b, (((ca,), (cb,)), ((), ())), preferred_element_type=F32)


def split(value):
    high = value.astype(BF)
    return high, (value - high.astype(F32)).astype(BF)


def kernel(
    q_ref, list_ref, pos_ref, p_ref, acc_ref, l_hbm,
    new_hbm, sums_ref, full_hbm,
    gq, gm, lab, lp, lt, total, rows, cp, cd, oh, mk, mc, pj, rb0, sb, rb1, rb2, rb3, s1, s2, g1, full,
    sem_l, sem_o, sem_f,
    qs, qr, ms, mr, bs, br, bms, bmr, rs, rr,
):
    y = lax.axis_index("group")
    s = lax.axis_index("shard")
    x, z, k = s // 8, (s // 2) % 4, s % 2
    here = (x, y, z)
    at = [[here[a] for a in order] for order in ORDERS]
    scale = 1.0 / math.sqrt(D)
    T3 = range(3)

    def device(c, core):
        return (c[1], (c[0] * 4 + c[2]) * 2 + core)

    def shifted(axis, r):
        c = list(here)
        c[axis] = (c[axis] + r) % 4
        return device(c, k)

    sibling = device(here, 1 - k)
    partner = [[shifted(axis, r) for r in (1, 2, 3)] for axis in range(3)]

    pending = []

    def remote(src, dst, ssem, rsem, target):
        pltpu.make_async_remote_copy(
            src_ref=src, dst_ref=dst, send_sem=ssem, recv_sem=rsem,
            device_id=target, device_id_type=MESH,
        ).start()
        pending.append((src, ssem))

    def arrived(dst, rsem):
        pltpu.make_async_remote_copy(
            src_ref=dst, dst_ref=dst, send_sem=rsem, recv_sem=rsem,
            device_id=sibling, device_id_type=MESH,
        ).wait_recv()

    def drain():
        for src, ssem in pending:
            pltpu.make_async_remote_copy(
                src_ref=src, dst_ref=src, send_sem=ssem, recv_sem=ssem,
                device_id=sibling, device_id_type=MESH,
            ).wait_send()
        pending.clear()

    barrier = pltpu.get_barrier_semaphore()
    for axis in range(3):
        for r in range(3):
            pl.semaphore_signal(barrier, inc=1, device_id=partner[axis][r], device_id_type=MESH)
    pl.semaphore_signal(barrier, inc=1, device_id=sibling, device_id_type=MESH)
    load = pltpu.make_async_copy(l_hbm, lab, sem_l)
    load.start()

    ids = list_ref[...]
    pos = pos_ref[...]

    codes = lax.shift_left(128 + (ids & 127), lax.shift_right_logical(ids, 7)).astype(F32)
    marks = jnp.concatenate(
        [
            (lax.shift_right_logical(pos, 8) + 1).astype(F32),
            ((pos & 255) + 1).astype(F32),
            jnp.zeros((8, QD), F32),
        ],
        axis=0,
    )
    for t, value in enumerate((codes[:16], codes[16:], marks)):
        gm[t, k, 0, 0, 0] = value.astype(BF)
    for t in T3:
        gq[t, k, 0, 0, 0] = q_ref[:, t * 256:(t + 1) * 256]
    total[...] = jnp.zeros_like(total)
    pl.semaphore_wait(barrier, 10)

    UNITS = (
        (0, 0, (0, 1)),
        (1, 0, (0, 1)), (1, 0, (1, 2)), (1, 0, (3, 1)),
        (2, 0, (0, 1)), (2, 0, (1, 2)), (2, 0, (3, 1)),
        (2, 1, (0, 4)), (2, 2, (0, 4)), (2, 3, (0, 4)),
    )

    def region(t, n, place):
        ring, j, (lo, size) = UNITS[n]
        if ring == 0:
            return gq.at[t, k, 0, 0, pl.ds(place, 1)]
        if ring == 1:
            return gq.at[t, k, 0, place, pl.ds(lo, size)]
        return gq.at[t, k, place, j, pl.ds(lo, size)]

    def half(ref, way):
        return ref.at[:, pl.ds(64 * way, 64)]

    def toward(t, n, way):
        return partner[ORDERS[t][UNITS[n][0]]][0 if way == 0 else 2]

    def both_ways(t, n):
        for way in (0, 1):
            remote(region(t, n, 0), region(t, n, 1 + way), qs.at[t, n, 0, way], qr.at[t, n, 0, way], toward(t, n, way))

    def onward(t, n, way):
        arrived(region(t, n, 1 + way), qr.at[t, n, 0, way])
        remote(
            half(region(t, n, 1 + way), way), half(region(t, n, 3), way),
            qs.at[t, n, 1, way], qr.at[t, n, 1, way], toward(t, n, way),
        )

    def far(t, n):
        for way in (0, 1):
            arrived(half(region(t, n, 3), way), qr.at[t, n, 1, way])

    def meta_region(t, ring, place):
        if ring == 0:
            return gm.at[t, k, 0, 0, place]
        if ring == 1:
            return gm.at[t, k, 0, place]
        return gm.at[t, k, place]

    def meta_send(ring):
        for t in T3:
            for r in (1, 2, 3):
                remote(
                    meta_region(t, ring, 0), meta_region(t, ring, PLACE[r]),
                    ms.at[t, ring, r - 1], mr.at[t, ring, r - 1], partner[ORDERS[t][ring]][r - 1],
                )

    def meta_wait(ring):
        for t in T3:
            for r in (1, 2, 3):
                arrived(meta_region(t, ring, PLACE[r]), mr.at[t, ring, r - 1])

    landed, shared = set(), set()

    def to_sibling(t, r3, j):
        ref = gq.at[t, k, r3, j]
        remote(ref, ref, bs.at[t, r3, j], br.at[t, r3, j], sibling)
        landed.add((t, r3, j))

    def require(group):
        lines = set()
        for o in CHIPS[group * GROUP:(group + 1) * GROUP]:
            for t in T3:
                lines.add((t, o[ORDERS[t][2]], o[ORDERS[t][1]]))
        assert lines <= landed
        for t, r3, j in sorted(lines - shared):
            arrived(gq.at[t, 1 - k, r3, j], br.at[t, r3, j])
        shared.update(lines)

    def meta_sibling(r3):
        for t in T3:
            ref = gm.at[t, k, r3]
            remote(ref, ref, bms.at[t, r3], bmr.at[t, r3], sibling)

    def prepare(c, _):
        here_l = pl.ds(pl.multiple_of(c * LBL, LBL), LBL)
        slab = lab[here_l, :]
        lp[here_l, :] = dot(slab, p_ref[...], 1, 1).astype(BF)
        lt[:, here_l] = slab.T
        return 0

    def prepare_some(lo, hi):
        lax.fori_loop(lo, hi, prepare, 0)

    number = y * 32 + s
    first = number * CL
    octave = first // 128
    base = (128 + first % 128).astype(F32)
    power = lax.shift_left(jnp.int32(1), octave.astype(jnp.int32)).astype(F32)

    def four_chips(group, step):
        words = []
        for h in range(4):
            word = 0
            for n in range(4):
                o = CHIPS[group * GROUP + h * 4 + n]
                word |= (o[0] + 4 * o[1] + 16 * o[2]) << (6 * n)
            words.append(word)
        word = jnp.where(step == 0, words[0], jnp.where(step == 1, words[1], jnp.where(step == 2, words[2], words[3])))
        places = []
        for n in range(4):
            code = (word // (1 << (6 * n))) % 64
            places.append((code % 4, (code // 4) % 4, code // 16))
        return places

    def pair(ref, c, t):
        a1, a2, a3 = ORDERS[t]
        return ref[t, 0, c[a3], c[a2], c[a1]], ref[t, 1, c[a3], c[a2], c[a1]]

    lane = lax.broadcasted_iota(jnp.int32, (16, 256), 1)
    sub = lax.broadcasted_iota(jnp.int32, (16, 256), 0)
    own_slot = jnp.where(sub // W == lane // QD, sub % W, -2).astype(F32)
    own_cluster = (
        lax.broadcasted_iota(jnp.int32, (CL, 128), 0) == lax.broadcasted_iota(jnp.int32, (CL, 128), 1) // 16
    )
    lane_chip = lax.broadcasted_iota(jnp.int32, (8, 128), 1) // 16
    before = lax.broadcasted_iota(jnp.int32, (256, 256), 0)
    after = lax.broadcasted_iota(jnp.int32, (256, 256), 1)
    tri = jnp.where((before < after) & (before // QD == after // QD), 1.0, 0.0).astype(BF)

    def pick(group):
        def names(step, _):
            for u, c in enumerate(four_chips(group, step)):
                a0, a1 = pair(gm, c, 0)
                b0, b1 = pair(gm, c, 1)
                ids = jnp.concatenate(
                    [jnp.concatenate([a0, b0], axis=0), jnp.concatenate([a1, b1], axis=0)], axis=1
                ).astype(F32)
                column = lax.broadcasted_iota(jnp.int32, (32, 256), 0).astype(F32) + 1.0
                found = []
                for n in range(CL):
                    found.append(jnp.sum(jnp.where(ids == (base + n) * power, column, 0.0), axis=0, keepdims=True))
                cp[pl.ds(pl.multiple_of(step * 4 * CL + u * CL, CL), CL), :] = jnp.concatenate(found, axis=0)
            return 0

        lax.fori_loop(0, GROUP // 4, names, 0)
        picked = cp[...] > 0.0
        rank = dot(jnp.where(picked, 1.0, 0.0).astype(BF), tri)
        cd[...] = jnp.where(picked, rank, -1.0)

        def hot(step, _):
            for u, c in enumerate(four_chips(group, step)):
                here_c = pl.ds(pl.multiple_of(step * 4 * CL + u * CL, CL), CL)
                code = cd[here_c, :]
                onehot = jnp.concatenate(
                    [jnp.where(code[n:n + 1, :] == own_slot, 1.0, 0.0).astype(BF) for n in range(CL)], axis=0
                )
                oh[group * GROUP + step * 4 + u] = onehot
                m0, m1 = pair(gm, c, 2)
                marks = jnp.concatenate([m0, m1], axis=1).astype(F32)
                column = cp[here_c, :]
                shifted_marks = jnp.concatenate(
                    [jnp.where(marks[n:n + 1, :] == column, marks[4 + n:5 + n, :], 0.0) for n in range(4)], axis=0
                ).astype(BF)
                spread = dot(shifted_marks, onehot, 1, 1)
                mk[step * 4 + u] = jnp.concatenate(
                    [
                        jnp.sum(jnp.where(own_cluster, spread[n * CL:(n + 1) * CL, :], 0.0), axis=0, keepdims=True)
                        for n in range(4)
                    ]
                    + [jnp.zeros((4, 128), F32)],
                    axis=0,
                )
            return 0

        lax.fori_loop(0, GROUP // 4, hot, 0)
        for h in range(GROUP // 8):
            for n in range(CL):
                line_marks = jnp.zeros((8, 128), F32)
                for i in range(8):
                    turned = pltpu.roll(mk[h * 8 + i], (16 * (i - n)) % 128, 1)
                    line_marks = jnp.where(lane_chip == i, turned, line_marks)
                mc[group, n, :, h * 128:(h + 1) * 128] = line_marks

    def gather_rows(group):
        def choose(step, _):
            for u, c in enumerate(four_chips(group, step)):
                onehot = oh[group * GROUP + step * 4 + u]
                at_row = pl.ds(pl.multiple_of(step * 64 + u * 16, 16), 16)
                for t in T3:
                    q0, q1 = pair(gq, c, t)
                    got = dot(onehot, jnp.concatenate([q0, q1], axis=0)).astype(BF)
                    for n in range(CL):
                        rows[n, at_row, t * 256:(t + 1) * 256] = got[n * 16:(n + 1) * 16, :]
            return 0

        lax.fori_loop(0, GROUP // 4, choose, 0, unroll=2)

    def sum_rows(group):
        def cluster(m0, _):
            label = lax.broadcasted_iota(jnp.int32, (LBL, GROUP * 16), 0).astype(F32) + 1.0

            def place(u):
                return pl.ds(pl.multiple_of((4 * m0 + u) * LBL, LBL), LBL)

            def scored(u):
                return dot(lp[place(u), :], rows[4 * m0 + u], 1, 1) * scale

            def signal(u, sc):
                m = mc[group, 4 * m0 + u]
                hit = (m[0:1] == label) | (m[1:2] == label) | (m[2:3] == label) | (m[3:4] == label)
                return (1.0 / (1.0 + jnp.exp(-sc)) - jnp.where(hit, 1.0, 0.0)).astype(BF)

            def add(u):
                summed = total[place(u), :] + dot(signals[u], rows[4 * m0 + u])
                total[place(u), :] = summed
                if group == GROUPS - 1:
                    rows[4 * m0 + u] = summed.astype(BF)

            scores, signals = [scored(0), scored(1)], []
            for u in range(4):
                signals.append(signal(u, scores[u]))
                if u + 2 < 4:
                    scores.append(scored(u + 2))
                if u > 0:
                    add(u - 1)
            add(3)
            return 0

        lax.fori_loop(0, CL // 4, cluster, 0)

    def group_work(group):
        gather_rows(group)
        sum_rows(group)

    def every(n, act):
        for t in T3:
            for way in (0, 1):
                act(t, n, way)

    def sharing(n, j):
        for t in T3:
            for way in (0, 1):
                onward(t, n, way)
                to_sibling(t, 1 + way, j)

    def far_after(ns, j, r3=3):
        for t in T3:
            for n in ns:
                far(t, n)
            to_sibling(t, r3, j)

    meta_send(0)
    for n in (0, 1, 4):
        for t in T3:
            both_ways(t, n)
    load.wait()
    prepare_some(0, 2)
    meta_wait(0)
    meta_send(1)
    for t in T3:
        for way in (0, 1):
            onward(t, 0, way)
        both_ways(t, 2)
    every(1, onward)
    every(4, onward)
    prepare_some(2, 4)
    meta_wait(1)
    meta_send(2)
    meta_sibling(0)
    for t in T3:
        far(t, 0)
        both_ways(t, 5)
        both_ways(t, 3)
        both_ways(t, 6)
        to_sibling(t, 0, 0)
    prepare_some(4, 8)
    every(2, onward)
    for t in T3:
        for way in (0, 1):
            onward(t, 3, way)
            to_sibling(t, 0, 1 + way)
        both_ways(t, 7)
    meta_wait(2)
    for r3 in (1, 2, 3):
        meta_sibling(r3)
    every(5, onward)
    for t in T3:
        for way in (0, 1):
            onward(t, 6, way)
            to_sibling(t, 1 + way, 0)
        both_ways(t, 8)
    for t in T3:
        for r3 in range(4):
            arrived(gm.at[t, 1 - k, r3], bmr.at[t, r3])
    pick(0)
    far_after((1, 2, 3), 3, 0)
    pick(1)
    for t in T3:
        for way in (0, 1):
            onward(t, 7, way)
            to_sibling(t, 1 + way, 1)
        both_ways(t, 9)
    pick(2)
    far_after((4, 5, 6), 0)
    require(0)
    gather_rows(0)
    sum_rows(0)
    sharing(8, 2)
    pick(3)
    far_after((7,), 1)
    require(1)
    gather_rows(1)
    sum_rows(1)
    sharing(9, 3)
    far_after((8,), 2)
    require(2)
    gather_rows(2)
    far_after((9,), 3)
    sum_rows(2)
    require(3)
    gather_rows(3)
    sum_rows(3)
    for t in T3:
        for r3 in range(4):
            for j in range(4):
                if (t, r3, j) not in shared:
                    arrived(gq.at[t, 1 - k, r3, j], br.at[t, r3, j])

    def project(which):
        at_half = pl.ds(pl.multiple_of(which * 384, 128), 384)
        for t in T3:
            for m in range(2):
                add = dot(lt[at_half, m * 1024:(m + 1) * 1024], rows[m * 4:(m + 1) * 4, :, t * 256:(t + 1) * 256].reshape(1024, 256))
                if m == 0:
                    pj[at_half, t * 256:(t + 1) * 256] = add
                else:
                    pj[at_half, t * 256:(t + 1) * 256] += add

    other_half = pl.ds(pl.multiple_of((1 - k) * 384, 128), 384)
    own_half = pl.ds(pl.multiple_of(k * 384, 128), 384)
    project(1 - k)
    remote(pj.at[other_half], rb0, rs.at[0], rr.at[0], sibling)
    project(k)

    eye = lax.broadcasted_iota(jnp.int32, (128, 128), 0) == lax.broadcasted_iota(jnp.int32, (128, 128), 1)

    def adagrad(n, _):
        here_l = pl.ds(pl.multiple_of(n * LBL, LBL), LBL)
        high, low = split(total[here_l, :])
        grad = (dot(high, p_ref[...]) + dot(low, p_ref[...])) * scale
        mean = jnp.sum(grad * grad, axis=1, keepdims=True) * (1.0 / D)
        old = jnp.concatenate(
            [
                jnp.sum(jnp.where(eye, acc_ref[pl.ds(n * 2 + h, 1), :], 0.0), axis=1, keepdims=True)
                for h in range(2)
            ],
            axis=0,
        )
        sums = old + mean
        for h in range(2):
            sums_ref[pl.ds(n * 2 + h, 1), :] = jnp.sum(
                jnp.where(eye, sums[h * 128:(h + 1) * 128], 0.0), axis=0, keepdims=True
            )
        rows[n] = (lab[here_l, :].astype(F32) - grad * (1.0 / jnp.sqrt(sums))).astype(BF)
        pltpu.make_async_copy(rows.at[n], new_hbm.at[here_l], sem_o.at[n]).start()
        return 0

    def adagrad_some(lo, hi):
        lax.fori_loop(lo, hi, adagrad, 0)

    arrived(rb0, rr.at[0])
    mine_sum = pj[own_half, :] + rb0[...]
    sb[...] = mine_sum.astype(BF)

    def cols(t):
        return pl.ds(t * 256, 256)

    def exchange(n, t, ring, src_of, dst_of):
        for r in (1, 2, 3):
            slot = 1 + n * 9 + t * 3 + r - 1
            remote(src_of(r), dst_of(r), rs.at[slot], rr.at[slot], partner[ORDERS[t][ring]][r - 1])

    def exchanged(n, t, ring, dst_of):
        for r in (1, 2, 3):
            slot = 1 + n * 9 + t * 3 + r - 1
            arrived(dst_of(r, (at[t][ring] - r + 4) % 4), rr.at[slot])

    def piece(i):
        return pl.ds(pl.multiple_of(i * 96, 32), 96)

    def full_piece(i):
        return pl.ds(pl.multiple_of(k * 384 + i * 96, 32), 96)

    def tiles(i):
        return pl.ds(i * 3, 3)

    def laid(r, l):
        return r * 2 + l, slice(r * 16, (r + 1) * 16), slice(l * 128, (l + 1) * 128)

    TILES = [laid(r, l) for r in range(6) for l in range(2)]

    for t in T3:
        exchange(0, t, 0, lambda r: sb.at[piece((at[t][0] + r) % 4), cols(t)], lambda r: rb1.at[t, r - 1])
    adagrad_some(0, 1)
    drain()
    for t in T3:
        exchanged(0, t, 0, lambda r, i: rb1.at[t, r - 1])
        summed = (
            (sb[piece(at[t][0]), cols(t)].astype(F32) + rb1[t, 0].astype(F32))
            + (rb1[t, 1].astype(F32) + rb1[t, 2].astype(F32))
        ).astype(BF)
        for n, down, across in TILES:
            s1[t, n] = summed[down, across]
        exchange(1, t, 1, lambda r: s1.at[t, tiles((at[t][1] + r) % 4)], lambda r: rb2.at[t, r - 1])
    adagrad_some(1, 3)
    for t in T3:
        exchanged(1, t, 1, lambda r, i: rb2.at[t, r - 1])
        s2[t] = (
            (s1[t, tiles(at[t][1])].astype(F32) + rb2[t, 0].astype(F32))
            + (rb2[t, 1].astype(F32) + rb2[t, 2].astype(F32))
        ).astype(BF)
        rb3[t, at[t][2]] = s2[t]
        exchange(2, t, 2, lambda r: s2.at[t], lambda r: rb3.at[t, at[t][2]])
    adagrad_some(3, 4)
    for t in T3:
        exchanged(2, t, 2, lambda r, i: rb3.at[t, i])
        mine = tiles(at[t][1])
        g1[t, mine] = (
            (rb3[t, 0].astype(F32) + rb3[t, 1].astype(F32)) + (rb3[t, 2].astype(F32) + rb3[t, 3].astype(F32))
        ).astype(BF)
        exchange(3, t, 1, lambda r: g1.at[t, mine], lambda r: g1.at[t, mine])
    adagrad_some(4, 5)

    def share_piece(t, r):
        ref = full.at[full_piece((at[t][0] - r + 4) % 4), cols(t)]
        remote(ref, ref, rs.at[46 + t * 4 + r], rr.at[46 + t * 4 + r], sibling)

    for t in T3:
        exchanged(3, t, 1, lambda r, i: g1.at[t, tiles(i)])
        summed = jnp.concatenate(
            [jnp.concatenate([g1[t, 2 * r], g1[t, 2 * r + 1]], axis=1) for r in range(6)], axis=0
        )
        mine = full.at[full_piece(at[t][0]), cols(t)]
        mine[...] = summed
        exchange(4, t, 0, lambda r: mine, lambda r: mine)
        share_piece(t, 0)
    adagrad_some(5, 7)
    for r in (1, 3, 2):
        for t in T3:
            slot = 1 + 4 * 9 + t * 3 + r - 1
            arrived(full.at[full_piece((at[t][0] - r + 4) % 4), cols(t)], rr.at[slot])
            share_piece(t, r)
    out_own = pltpu.make_async_copy(full.at[own_half], full_hbm.at[own_half], sem_f.at[0])
    out_own.start()
    adagrad_some(7, 8)
    for t in T3:
        for r in range(4):
            i = (at[t][0] - r + 4) % 4
            arrived(full.at[pl.ds(pl.multiple_of((1 - k) * 384 + i * 96, 32), 96), cols(t)], rr.at[46 + t * 4 + r])
    out_other = pltpu.make_async_copy(full.at[other_half], full_hbm.at[other_half], sem_f.at[1])
    out_other.start()
    for n in range(CL):
        pltpu.make_async_copy(rows.at[n], new_hbm.at[pl.ds(n * LBL, LBL)], sem_o.at[n]).wait()
    drain()
    out_own.wait()
    out_other.wait()


def finish(new_hbm, sums_ref, full_ref, labels_hbm, acc_ref, grad_ref, held, sem_in, sem_out):
    parts = [pl.ds(n * LBL, LBL) for n in range(CL)]
    ins = [pltpu.make_async_copy(new_hbm.at[p], held.at[p], sem_in.at[n]) for n, p in enumerate(parts)]
    outs = [pltpu.make_async_copy(held.at[p], labels_hbm.at[p], sem_out.at[n]) for n, p in enumerate(parts)]
    for copy in ins:
        copy.start()
    acc_ref[...] = sums_ref[...]
    scale = 1.0 / math.sqrt(D)
    wide = full_ref[...].astype(F32)
    squares = jnp.sum(wide * wide, keepdims=True) * (scale * scale)
    factor = jnp.minimum(1.0, D / jnp.sqrt(squares + 1e-06)) * scale
    for n in range(CL):
        ins[n].wait()
        outs[n].start()
    for n in range(D // 128):
        grad_ref[:, n * 128:(n + 1) * 128] = full_ref[n * 128:(n + 1) * 128, :].astype(F32).T * factor
    for copy in outs:
        copy.wait()


def on_device(queries, projection, labels, accumulator, shortlist, positives):
    vmem = pl.BlockSpec(memory_space=pltpu.VMEM)
    hbm = pl.BlockSpec(memory_space=pl.ANY)
    dma = pltpu.SemaphoreType.DMA
    new_labels, sums, proj = pl.pallas_call(
        kernel,
        out_shape=(
            jax.ShapeDtypeStruct((CL * LBL, D), BF),
            jax.ShapeDtypeStruct((16, 128), F32),
            jax.ShapeDtypeStruct((D, D), BF),
        ),
        in_specs=[vmem] * 5 + [hbm],
        out_specs=(hbm, vmem, hbm),
        scratch_shapes=[
            pltpu.VMEM((3, 2, 4, 4, 4, QD, 256), BF),
            pltpu.VMEM((3, 2, 4, 4, 4, 16, QD), BF),
            pltpu.VMEM((CL * LBL, D), BF),
            pltpu.VMEM((CL * LBL, D), BF),
            pltpu.VMEM((D, CL * LBL), BF),
            pltpu.VMEM((CL * LBL, D), F32),
            pltpu.VMEM((CL, GROUP * 16, D), BF),
            pltpu.VMEM((GROUP * CL, 256), F32),
            pltpu.VMEM((GROUP * CL, 256), F32),
            pltpu.VMEM((64, 128, 256), BF),
            pltpu.VMEM((GROUP, 8, 128), F32),
            pltpu.VMEM((GROUPS, CL, 8, GROUP * 16), F32),
            pltpu.VMEM((D, D), F32),
            pltpu.VMEM((384, D), F32),
            pltpu.VMEM((384, D), BF),
            pltpu.VMEM((3, 3, 96, 256), BF),
            pltpu.VMEM((3, 3, 3, 16, 128), BF),
            pltpu.VMEM((3, 4, 3, 16, 128), BF),
            pltpu.VMEM((3, 12, 16, 128), BF),
            pltpu.VMEM((3, 3, 16, 128), BF),
            pltpu.VMEM((3, 12, 16, 128), BF),
            pltpu.VMEM((D, D), BF),
            dma, dma((CL,)), dma((2,)),
            dma((3, 10, 2, 2)), dma((3, 10, 2, 2)),
            dma((3, 3, 3)), dma((3, 3, 3)),
            dma((3, 4, 4)), dma((3, 4, 4)),
            dma((3, 4)), dma((3, 4)),
            dma((58,)), dma((58,)),
        ],
        compiler_params=pltpu.CompilerParams(
            collective_id=0, has_side_effects=True, vmem_limit_bytes=63 * 1024 * 1024
        ),
        cost_estimate=pl.CostEstimate(flops=20 * 10**9, bytes_accessed=20 * 10**6, transcendentals=0),
    )(queries, shortlist.T, positives.T, projection, accumulator.reshape(16, 128), labels)
    labels_out, sums_out, grad = pl.pallas_call(
        finish,
        out_shape=(
            jax.ShapeDtypeStruct((CL * LBL, D), BF),
            jax.ShapeDtypeStruct((16, 128), F32),
            jax.ShapeDtypeStruct((D, D), F32),
        ),
        in_specs=[hbm, vmem, vmem],
        out_specs=(hbm, vmem, vmem),
        scratch_shapes=[pltpu.VMEM((CL * LBL, D), BF), dma((CL,)), dma((CL,))],
    )(new_labels, sums, proj)
    return labels_out, sums_out.reshape(-1), grad


def solution(mesh):
    in_specs = (
        P(("group", "shard"), None),
        P(),
        P(("group", "shard"), None),
        P(("group", "shard")),
        P(("group", "shard"), None),
        P(("group", "shard"), None),
    )
    out_specs = (P(("group", "shard"), None), P(("group", "shard")), P())
    return jax.shard_map(
        on_device, mesh=mesh, in_specs=in_specs, out_specs=out_specs, check_vma=False
    )
```

```python
import functools
import math

import jax
import jax.numpy as jnp
from jax import lax
from jax.experimental import pallas as pl
from jax.experimental.pallas import tpu as pltpu
from jax.sharding import PartitionSpec as P

MESH = pl.DeviceIdType.MESH
LBL = 256
QD = 128
D = 768
CL = 8
W = 8
BF = jnp.bfloat16
F32 = jnp.float32
ORDERS = ((0, 1, 2), (1, 2, 0), (2, 0, 1))
PLACE = {1: 1, 2: 3, 3: 2}
GROUP = 16
GROUPS = 4


def arrival(place):
    worst = 0
    for order in ORDERS:
        third, second = place[order[2]], place[order[1]]
        tick = ((0, 0, 0, 0), (1, 2, 4, 6), (1, 2, 4, 6), (3, 5, 7, 8))[third][second]
        worst = max(worst, tick)
    return worst


CHIPS = sorted(
    [(a, b, c) for a in range(4) for b in range(4) for c in range(4)],
    key=lambda o: (arrival(o), o),
)


def dot(a, b, ca=1, cb=0):
    return lax.dot_general(a, b, (((ca,), (cb,)), ((), ())), preferred_element_type=F32)


def split(value):
    high = value.astype(BF)
    return high, (value - high.astype(F32)).astype(BF)


def kernel(
    q_ref, list_ref, pos_ref, p_ref, acc_ref, l_hbm,
    new_hbm, sums_ref, full_hbm,
    gq, gm, lab, lp, lt, total, rows, cp, cd, oh, mk, mc, pj, rb0, sb, rb1, rb2, rb3, s1, s2, g1, full,
    sem_l, sem_o, sem_f,
    qs, qr, ms, mr, bs, br, bms, bmr, rs, rr,
):
    y = lax.axis_index("group")
    s = lax.axis_index("shard")
    x, z, k = s // 8, (s // 2) % 4, s % 2
    here = (x, y, z)
    at = [[here[a] for a in order] for order in ORDERS]
    scale = 1.0 / math.sqrt(D)
    T3 = range(3)

    def device(c, core):
        return (c[1], (c[0] * 4 + c[2]) * 2 + core)

    def shifted(axis, r):
        c = list(here)
        c[axis] = (c[axis] + r) % 4
        return device(c, k)

    sibling = device(here, 1 - k)
    partner = [[shifted(axis, r) for r in (1, 2, 3)] for axis in range(3)]

    pending = []

    def remote(src, dst, ssem, rsem, target):
        pltpu.make_async_remote_copy(
            src_ref=src, dst_ref=dst, send_sem=ssem, recv_sem=rsem,
            device_id=target, device_id_type=MESH,
        ).start()
        pending.append((src, ssem))

    def arrived(dst, rsem):
        pltpu.make_async_remote_copy(
            src_ref=dst, dst_ref=dst, send_sem=rsem, recv_sem=rsem,
            device_id=sibling, device_id_type=MESH,
        ).wait_recv()

    def drain():
        for src, ssem in pending:
            pltpu.make_async_remote_copy(
                src_ref=src, dst_ref=src, send_sem=ssem, recv_sem=ssem,
                device_id=sibling, device_id_type=MESH,
            ).wait_send()
        pending.clear()

    barrier = pltpu.get_barrier_semaphore()
    for axis in range(3):
        for r in range(3):
            pl.semaphore_signal(barrier, inc=1, device_id=partner[axis][r], device_id_type=MESH)
    pl.semaphore_signal(barrier, inc=1, device_id=sibling, device_id_type=MESH)
    load = pltpu.make_async_copy(l_hbm, lab, sem_l)
    load.start()

    ids = list_ref[...]
    pos = pos_ref[...]

    codes = lax.shift_left(128 + (ids & 127), lax.shift_right_logical(ids, 7)).astype(F32)
    marks = jnp.concatenate(
        [
            (lax.shift_right_logical(pos, 8) + 1).astype(F32),
            ((pos & 255) + 1).astype(F32),
            jnp.zeros((8, QD), F32),
        ],
        axis=0,
    )
    for t, value in enumerate((codes[:16], codes[16:], marks)):
        gm[t, k, 0, 0, 0] = value.astype(BF)
    for t in T3:
        gq[t, k, 0, 0, 0] = q_ref[:, t * 256:(t + 1) * 256]
    total[...] = jnp.zeros_like(total)
    pl.semaphore_wait(barrier, 10)

    UNITS = (
        (0, 0, (0, 1)),
        (1, 0, (0, 1)), (1, 0, (1, 2)), (1, 0, (3, 1)),
        (2, 0, (0, 1)), (2, 0, (1, 2)), (2, 0, (3, 1)),
        (2, 1, (0, 4)), (2, 2, (0, 4)), (2, 3, (0, 4)),
    )

    def region(t, n, place):
        ring, j, (lo, size) = UNITS[n]
        if ring == 0:
            return gq.at[t, k, 0, 0, pl.ds(place, 1)]
        if ring == 1:
            return gq.at[t, k, 0, place, pl.ds(lo, size)]
        return gq.at[t, k, place, j, pl.ds(lo, size)]

    def half(ref, way):
        return ref.at[:, pl.ds(64 * way, 64)]

    def toward(t, n, way):
        return partner[ORDERS[t][UNITS[n][0]]][0 if way == 0 else 2]

    def both_ways(t, n):
        for way in (0, 1):
            remote(region(t, n, 0), region(t, n, 1 + way), qs.at[t, n, 0, way], qr.at[t, n, 0, way], toward(t, n, way))

    def onward(t, n, way):
        arrived(region(t, n, 1 + way), qr.at[t, n, 0, way])
        remote(
            half(region(t, n, 1 + way), way), half(region(t, n, 3), way),
            qs.at[t, n, 1, way], qr.at[t, n, 1, way], toward(t, n, way),
        )

    def far(t, n):
        for way in (0, 1):
            arrived(half(region(t, n, 3), way), qr.at[t, n, 1, way])

    def meta_region(t, ring, place):
        if ring == 0:
            return gm.at[t, k, 0, 0, place]
        if ring == 1:
            return gm.at[t, k, 0, place]
        return gm.at[t, k, place]

    def meta_send(ring):
        for t in T3:
            for r in (1, 2, 3):
                remote(
                    meta_region(t, ring, 0), meta_region(t, ring, PLACE[r]),
                    ms.at[t, ring, r - 1], mr.at[t, ring, r - 1], partner[ORDERS[t][ring]][r - 1],
                )

    def meta_wait(ring):
        for t in T3:
            for r in (1, 2, 3):
                arrived(meta_region(t, ring, PLACE[r]), mr.at[t, ring, r - 1])

    landed, shared = set(), set()

    def to_sibling(t, r3, j):
        ref = gq.at[t, k, r3, j]
        remote(ref, ref, bs.at[t, r3, j], br.at[t, r3, j], sibling)
        landed.add((t, r3, j))

    def require(group):
        lines = set()
        for o in CHIPS[group * GROUP:(group + 1) * GROUP]:
            for t in T3:
                lines.add((t, o[ORDERS[t][2]], o[ORDERS[t][1]]))
        assert lines <= landed
        for t, r3, j in sorted(lines - shared):
            arrived(gq.at[t, 1 - k, r3, j], br.at[t, r3, j])
        shared.update(lines)

    def meta_sibling(r3):
        for t in T3:
            ref = gm.at[t, k, r3]
            remote(ref, ref, bms.at[t, r3], bmr.at[t, r3], sibling)

    def prepare(c, _):
        here_l = pl.ds(pl.multiple_of(c * LBL, LBL), LBL)
        slab = lab[here_l, :]
        lp[here_l, :] = dot(slab, p_ref[...], 1, 1).astype(BF)
        lt[:, here_l] = slab.T
        return 0

    def prepare_some(lo, hi):
        lax.fori_loop(lo, hi, prepare, 0)

    number = y * 32 + s
    first = number * CL
    octave = first // 128
    base = (128 + first % 128).astype(F32)
    power = lax.shift_left(jnp.int32(1), octave.astype(jnp.int32)).astype(F32)

    def four_chips(group, step):
        words = []
        for h in range(4):
            word = 0
            for n in range(4):
                o = CHIPS[group * GROUP + h * 4 + n]
                word |= (o[0] + 4 * o[1] + 16 * o[2]) << (6 * n)
            words.append(word)
        word = jnp.where(step == 0, words[0], jnp.where(step == 1, words[1], jnp.where(step == 2, words[2], words[3])))
        places = []
        for n in range(4):
            code = (word // (1 << (6 * n))) % 64
            places.append((code % 4, (code // 4) % 4, code // 16))
        return places

    def pair(ref, c, t):
        a1, a2, a3 = ORDERS[t]
        return ref[t, 0, c[a3], c[a2], c[a1]], ref[t, 1, c[a3], c[a2], c[a1]]

    lane = lax.broadcasted_iota(jnp.int32, (16, 256), 1)
    sub = lax.broadcasted_iota(jnp.int32, (16, 256), 0)
    own_slot = jnp.where(sub // W == lane // QD, sub % W, -2).astype(F32)
    own_cluster = (
        lax.broadcasted_iota(jnp.int32, (CL, 128), 0) == lax.broadcasted_iota(jnp.int32, (CL, 128), 1) // 16
    )
    lane_chip = lax.broadcasted_iota(jnp.int32, (8, 128), 1) // 16
    before = lax.broadcasted_iota(jnp.int32, (256, 256), 0)
    after = lax.broadcasted_iota(jnp.int32, (256, 256), 1)
    tri = jnp.where((before < after) & (before // QD == after // QD), 1.0, 0.0).astype(BF)

    def pick(group):
        def names(step, _):
            for u, c in enumerate(four_chips(group, step)):
                a0, a1 = pair(gm, c, 0)
                b0, b1 = pair(gm, c, 1)
                ids = jnp.concatenate(
                    [jnp.concatenate([a0, b0], axis=0), jnp.concatenate([a1, b1], axis=0)], axis=1
                ).astype(F32)
                column = lax.broadcasted_iota(jnp.int32, (32, 256), 0).astype(F32) + 1.0
                found = []
                for n in range(CL):
                    found.append(jnp.sum(jnp.where(ids == (base + n) * power, column, 0.0), axis=0, keepdims=True))
                cp[pl.ds(pl.multiple_of(step * 4 * CL + u * CL, CL), CL), :] = jnp.concatenate(found, axis=0)
            return 0

        lax.fori_loop(0, GROUP // 4, names, 0, unroll=2)
        picked = cp[...] > 0.0
        rank = dot(jnp.where(picked, 1.0, 0.0).astype(BF), tri)
        cd[...] = jnp.where(picked, rank, -1.0)

        def hot(step, _):
            for u, c in enumerate(four_chips(group, step)):
                here_c = pl.ds(pl.multiple_of(step * 4 * CL + u * CL, CL), CL)
                code = cd[here_c, :]
                onehot = jnp.concatenate(
                    [jnp.where(code[n:n + 1, :] == own_slot, 1.0, 0.0).astype(BF) for n in range(CL)], axis=0
                )
                oh[group * GROUP + step * 4 + u] = onehot
                m0, m1 = pair(gm, c, 2)
                marks = jnp.concatenate([m0, m1], axis=1).astype(F32)
                column = cp[here_c, :]
                shifted_marks = jnp.concatenate(
                    [jnp.where(marks[n:n + 1, :] == column, marks[4 + n:5 + n, :], 0.0) for n in range(4)], axis=0
                ).astype(BF)
                spread = dot(shifted_marks, onehot, 1, 1)
                mk[step * 4 + u] = jnp.concatenate(
                    [
                        jnp.sum(jnp.where(own_cluster, spread[n * CL:(n + 1) * CL, :], 0.0), axis=0, keepdims=True)
                        for n in range(4)
                    ]
                    + [jnp.zeros((4, 128), F32)],
                    axis=0,
                )
            return 0

        lax.fori_loop(0, GROUP // 4, hot, 0, unroll=2)
        for h in range(GROUP // 8):
            for n in range(CL):
                line_marks = jnp.zeros((8, 128), F32)
                for i in range(8):
                    turned = pltpu.roll(mk[h * 8 + i], (16 * (i - n)) % 128, 1)
                    line_marks = jnp.where(lane_chip == i, turned, line_marks)
                mc[group, n, :, h * 128:(h + 1) * 128] = line_marks

    def gather_rows(group):
        def choose(step, _):
            for u, c in enumerate(four_chips(group, step)):
                onehot = oh[group * GROUP + step * 4 + u]
                at_row = pl.ds(pl.multiple_of(step * 64 + u * 16, 16), 16)
                for t in T3:
                    q0, q1 = pair(gq, c, t)
                    got = dot(onehot, jnp.concatenate([q0, q1], axis=0)).astype(BF)
                    for n in range(CL):
                        rows[n, at_row, t * 256:(t + 1) * 256] = got[n * 16:(n + 1) * 16, :]
            return 0

        lax.fori_loop(0, GROUP // 4, choose, 0, unroll=2)

    def sum_rows(group):
        def cluster(m0, _):
            label = lax.broadcasted_iota(jnp.int32, (LBL, GROUP * 16), 0).astype(F32) + 1.0

            def place(u):
                return pl.ds(pl.multiple_of((4 * m0 + u) * LBL, LBL), LBL)

            def scored(u):
                return dot(lp[place(u), :], rows[4 * m0 + u], 1, 1) * scale

            def signal(u, sc):
                m = mc[group, 4 * m0 + u]
                hit = (m[0:1] == label) | (m[1:2] == label) | (m[2:3] == label) | (m[3:4] == label)
                return (1.0 / (1.0 + jnp.exp(-sc)) - jnp.where(hit, 1.0, 0.0)).astype(BF)

            def add(u):
                summed = total[place(u), :] + dot(signals[u], rows[4 * m0 + u])
                total[place(u), :] = summed
                if group == GROUPS - 1:
                    rows[4 * m0 + u] = summed.astype(BF)

            scores, signals = [scored(0), scored(1)], []
            for u in range(4):
                signals.append(signal(u, scores[u]))
                if u + 2 < 4:
                    scores.append(scored(u + 2))
                if u > 0:
                    add(u - 1)
            add(3)
            return 0

        lax.fori_loop(0, CL // 4, cluster, 0, unroll=2)

    def group_work(group):
        gather_rows(group)
        sum_rows(group)

    def every(n, act):
        for t in T3:
            for way in (0, 1):
                act(t, n, way)

    def sharing(n, j):
        for t in T3:
            for way in (0, 1):
                onward(t, n, way)
                to_sibling(t, 1 + way, j)

    def far_after(ns, j, r3=3):
        for t in T3:
            for n in ns:
                far(t, n)
            to_sibling(t, r3, j)

    meta_send(0)
    for n in (0, 1, 4):
        for t in T3:
            both_ways(t, n)
    load.wait()
    prepare_some(0, 2)
    meta_wait(0)
    meta_send(1)
    for t in T3:
        for way in (0, 1):
            onward(t, 0, way)
        both_ways(t, 2)
    every(1, onward)
    every(4, onward)
    prepare_some(2, 4)
    meta_wait(1)
    meta_send(2)
    meta_sibling(0)
    for t in T3:
        far(t, 0)
        both_ways(t, 5)
        both_ways(t, 3)
        both_ways(t, 6)
        to_sibling(t, 0, 0)
    prepare_some(4, 8)
    every(2, onward)
    for t in T3:
        for way in (0, 1):
            onward(t, 3, way)
            to_sibling(t, 0, 1 + way)
        both_ways(t, 7)
    meta_wait(2)
    for r3 in (1, 2, 3):
        meta_sibling(r3)
    every(5, onward)
    for t in T3:
        for way in (0, 1):
            onward(t, 6, way)
            to_sibling(t, 1 + way, 0)
        both_ways(t, 8)
    for t in T3:
        for r3 in range(4):
            arrived(gm.at[t, 1 - k, r3], bmr.at[t, r3])
    pick(0)
    far_after((1, 2, 3), 3, 0)
    pick(1)
    for t in T3:
        for way in (0, 1):
            onward(t, 7, way)
            to_sibling(t, 1 + way, 1)
        both_ways(t, 9)
    pick(2)
    far_after((4, 5, 6), 0)
    require(0)
    gather_rows(0)
    sum_rows(0)
    sharing(8, 2)
    pick(3)
    far_after((7,), 1)
    require(1)
    gather_rows(1)
    sum_rows(1)
    sharing(9, 3)
    far_after((8,), 2)
    require(2)
    gather_rows(2)
    far_after((9,), 3)
    sum_rows(2)
    require(3)
    gather_rows(3)
    sum_rows(3)
    for t in T3:
        for r3 in range(4):
            for j in range(4):
                if (t, r3, j) not in shared:
                    arrived(gq.at[t, 1 - k, r3, j], br.at[t, r3, j])

    def project(which):
        at_half = pl.ds(pl.multiple_of(which * 384, 128), 384)
        for t in T3:
            for m in range(2):
                add = dot(lt[at_half, m * 1024:(m + 1) * 1024], rows[m * 4:(m + 1) * 4, :, t * 256:(t + 1) * 256].reshape(1024, 256))
                if m == 0:
                    pj[at_half, t * 256:(t + 1) * 256] = add
                else:
                    pj[at_half, t * 256:(t + 1) * 256] += add

    other_half = pl.ds(pl.multiple_of((1 - k) * 384, 128), 384)
    own_half = pl.ds(pl.multiple_of(k * 384, 128), 384)
    project(1 - k)
    remote(pj.at[other_half], rb0, rs.at[0], rr.at[0], sibling)
    project(k)

    eye = lax.broadcasted_iota(jnp.int32, (128, 128), 0) == lax.broadcasted_iota(jnp.int32, (128, 128), 1)

    def adagrad(n, _):
        here_l = pl.ds(pl.multiple_of(n * LBL, LBL), LBL)
        high, low = split(total[here_l, :])
        grad = (dot(high, p_ref[...]) + dot(low, p_ref[...])) * scale
        mean = jnp.sum(grad * grad, axis=1, keepdims=True) * (1.0 / D)
        old = jnp.concatenate(
            [
                jnp.sum(jnp.where(eye, acc_ref[pl.ds(n * 2 + h, 1), :], 0.0), axis=1, keepdims=True)
                for h in range(2)
            ],
            axis=0,
        )
        sums = old + mean
        for h in range(2):
            sums_ref[pl.ds(n * 2 + h, 1), :] = jnp.sum(
                jnp.where(eye, sums[h * 128:(h + 1) * 128], 0.0), axis=0, keepdims=True
            )
        rows[n] = (lab[here_l, :].astype(F32) - grad * (1.0 / jnp.sqrt(sums))).astype(BF)
        pltpu.make_async_copy(rows.at[n], new_hbm.at[here_l], sem_o.at[n]).start()
        return 0

    def adagrad_some(lo, hi):
        lax.fori_loop(lo, hi, adagrad, 0)

    arrived(rb0, rr.at[0])
    mine_sum = pj[own_half, :] + rb0[...]
    sb[...] = mine_sum.astype(BF)

    def cols(t):
        return pl.ds(t * 256, 256)

    def exchange(n, t, ring, src_of, dst_of):
        for r in (1, 2, 3):
            slot = 1 + n * 9 + t * 3 + r - 1
            remote(src_of(r), dst_of(r), rs.at[slot], rr.at[slot], partner[ORDERS[t][ring]][r - 1])

    def exchanged(n, t, ring, dst_of):
        for r in (1, 2, 3):
            slot = 1 + n * 9 + t * 3 + r - 1
            arrived(dst_of(r, (at[t][ring] - r + 4) % 4), rr.at[slot])

    def piece(i):
        return pl.ds(pl.multiple_of(i * 96, 32), 96)

    def full_piece(i):
        return pl.ds(pl.multiple_of(k * 384 + i * 96, 32), 96)

    def tiles(i):
        return pl.ds(i * 3, 3)

    def laid(r, l):
        return r * 2 + l, slice(r * 16, (r + 1) * 16), slice(l * 128, (l + 1) * 128)

    TILES = [laid(r, l) for r in range(6) for l in range(2)]

    for t in T3:
        exchange(0, t, 0, lambda r: sb.at[piece((at[t][0] + r) % 4), cols(t)], lambda r: rb1.at[t, r - 1])
    adagrad_some(0, 1)
    drain()
    for t in T3:
        exchanged(0, t, 0, lambda r, i: rb1.at[t, r - 1])
        summed = (
            (sb[piece(at[t][0]), cols(t)].astype(F32) + rb1[t, 0].astype(F32))
            + (rb1[t, 1].astype(F32) + rb1[t, 2].astype(F32))
        ).astype(BF)
        for n, down, across in TILES:
            s1[t, n] = summed[down, across]
        exchange(1, t, 1, lambda r: s1.at[t, tiles((at[t][1] + r) % 4)], lambda r: rb2.at[t, r - 1])
    adagrad_some(1, 3)
    for t in T3:
        exchanged(1, t, 1, lambda r, i: rb2.at[t, r - 1])
        s2[t] = (
            (s1[t, tiles(at[t][1])].astype(F32) + rb2[t, 0].astype(F32))
            + (rb2[t, 1].astype(F32) + rb2[t, 2].astype(F32))
        ).astype(BF)
        rb3[t, at[t][2]] = s2[t]
        exchange(2, t, 2, lambda r: s2.at[t], lambda r: rb3.at[t, at[t][2]])
    adagrad_some(3, 4)
    for t in T3:
        exchanged(2, t, 2, lambda r, i: rb3.at[t, i])
        mine = tiles(at[t][1])
        g1[t, mine] = (
            (rb3[t, 0].astype(F32) + rb3[t, 1].astype(F32)) + (rb3[t, 2].astype(F32) + rb3[t, 3].astype(F32))
        ).astype(BF)
        exchange(3, t, 1, lambda r: g1.at[t, mine], lambda r: g1.at[t, mine])
    adagrad_some(4, 5)

    def share_piece(t, r):
        ref = full.at[full_piece((at[t][0] - r + 4) % 4), cols(t)]
        remote(ref, ref, rs.at[46 + t * 4 + r], rr.at[46 + t * 4 + r], sibling)

    for t in T3:
        exchanged(3, t, 1, lambda r, i: g1.at[t, tiles(i)])
        summed = jnp.concatenate(
            [jnp.concatenate([g1[t, 2 * r], g1[t, 2 * r + 1]], axis=1) for r in range(6)], axis=0
        )
        mine = full.at[full_piece(at[t][0]), cols(t)]
        mine[...] = summed
        exchange(4, t, 0, lambda r: mine, lambda r: mine)
        share_piece(t, 0)
    adagrad_some(5, 7)
    for r in (1, 3, 2):
        for t in T3:
            slot = 1 + 4 * 9 + t * 3 + r - 1
            arrived(full.at[full_piece((at[t][0] - r + 4) % 4), cols(t)], rr.at[slot])
            share_piece(t, r)
    out_own = pltpu.make_async_copy(full.at[own_half], full_hbm.at[own_half], sem_f.at[0])
    out_own.start()
    adagrad_some(7, 8)
    for t in T3:
        for r in range(4):
            i = (at[t][0] - r + 4) % 4
            arrived(full.at[pl.ds(pl.multiple_of((1 - k) * 384 + i * 96, 32), 96), cols(t)], rr.at[46 + t * 4 + r])
    out_other = pltpu.make_async_copy(full.at[other_half], full_hbm.at[other_half], sem_f.at[1])
    out_other.start()
    for n in range(CL):
        pltpu.make_async_copy(rows.at[n], new_hbm.at[pl.ds(n * LBL, LBL)], sem_o.at[n]).wait()
    drain()
    out_own.wait()
    out_other.wait()


def finish(new_hbm, sums_ref, full_ref, labels_hbm, acc_ref, grad_ref, held, sem_in, sem_out):
    parts = [pl.ds(n * LBL, LBL) for n in range(CL)]
    ins = [pltpu.make_async_copy(new_hbm.at[p], held.at[p], sem_in.at[n]) for n, p in enumerate(parts)]
    outs = [pltpu.make_async_copy(held.at[p], labels_hbm.at[p], sem_out.at[n]) for n, p in enumerate(parts)]
    for copy in ins:
        copy.start()
    acc_ref[...] = sums_ref[...]
    scale = 1.0 / math.sqrt(D)
    wide = full_ref[...].astype(F32)
    squares = jnp.sum(wide * wide, keepdims=True) * (scale * scale)
    factor = jnp.minimum(1.0, D / jnp.sqrt(squares + 1e-06)) * scale
    for n in range(CL):
        ins[n].wait()
        outs[n].start()
    for n in range(D // 128):
        grad_ref[:, n * 128:(n + 1) * 128] = full_ref[n * 128:(n + 1) * 128, :].astype(F32).T * factor
    for copy in outs:
        copy.wait()


def on_device(queries, projection, labels, accumulator, shortlist, positives):
    vmem = pl.BlockSpec(memory_space=pltpu.VMEM)
    hbm = pl.BlockSpec(memory_space=pl.ANY)
    dma = pltpu.SemaphoreType.DMA
    new_labels, sums, proj = pl.pallas_call(
        kernel,
        out_shape=(
            jax.ShapeDtypeStruct((CL * LBL, D), BF),
            jax.ShapeDtypeStruct((16, 128), F32),
            jax.ShapeDtypeStruct((D, D), BF),
        ),
        in_specs=[vmem] * 5 + [hbm],
        out_specs=(hbm, vmem, hbm),
        scratch_shapes=[
            pltpu.VMEM((3, 2, 4, 4, 4, QD, 256), BF),
            pltpu.VMEM((3, 2, 4, 4, 4, 16, QD), BF),
            pltpu.VMEM((CL * LBL, D), BF),
            pltpu.VMEM((CL * LBL, D), BF),
            pltpu.VMEM((D, CL * LBL), BF),
            pltpu.VMEM((CL * LBL, D), F32),
            pltpu.VMEM((CL, GROUP * 16, D), BF),
            pltpu.VMEM((GROUP * CL, 256), F32),
            pltpu.VMEM((GROUP * CL, 256), F32),
            pltpu.VMEM((64, 128, 256), BF),
            pltpu.VMEM((GROUP, 8, 128), F32),
            pltpu.VMEM((GROUPS, CL, 8, GROUP * 16), F32),
            pltpu.VMEM((D, D), F32),
            pltpu.VMEM((384, D), F32),
            pltpu.VMEM((384, D), BF),
            pltpu.VMEM((3, 3, 96, 256), BF),
            pltpu.VMEM((3, 3, 3, 16, 128), BF),
            pltpu.VMEM((3, 4, 3, 16, 128), BF),
            pltpu.VMEM((3, 12, 16, 128), BF),
            pltpu.VMEM((3, 3, 16, 128), BF),
            pltpu.VMEM((3, 12, 16, 128), BF),
            pltpu.VMEM((D, D), BF),
            dma, dma((CL,)), dma((2,)),
            dma((3, 10, 2, 2)), dma((3, 10, 2, 2)),
            dma((3, 3, 3)), dma((3, 3, 3)),
            dma((3, 4, 4)), dma((3, 4, 4)),
            dma((3, 4)), dma((3, 4)),
            dma((58,)), dma((58,)),
        ],
        compiler_params=pltpu.CompilerParams(
            collective_id=0, has_side_effects=True, vmem_limit_bytes=63 * 1024 * 1024
        ),
        cost_estimate=pl.CostEstimate(flops=20 * 10**9, bytes_accessed=20 * 10**6, transcendentals=0),
    )(queries, shortlist.T, positives.T, projection, accumulator.reshape(16, 128), labels)
    labels_out, sums_out, grad = pl.pallas_call(
        finish,
        out_shape=(
            jax.ShapeDtypeStruct((CL * LBL, D), BF),
            jax.ShapeDtypeStruct((16, 128), F32),
            jax.ShapeDtypeStruct((D, D), F32),
        ),
        in_specs=[hbm, vmem, vmem],
        out_specs=(hbm, vmem, vmem),
        scratch_shapes=[pltpu.VMEM((CL * LBL, D), BF), dma((CL,)), dma((CL,))],
    )(new_labels, sums, proj)
    return labels_out, sums_out.reshape(-1), grad


def solution(mesh):
    in_specs = (
        P(("group", "shard"), None),
        P(),
        P(("group", "shard"), None),
        P(("group", "shard")),
        P(("group", "shard"), None),
        P(("group", "shard"), None),
    )
    out_specs = (P(("group", "shard"), None), P(("group", "shard")), P())
    return jax.shard_map(
        on_device, mesh=mesh, in_specs=in_specs, out_specs=out_specs, check_vma=False
    )
```
